32 devices in a mesh: qry: 8 (over z, core), lib: 4 (over y, x).
Axes of the slice: x: 2, y: 2, z: 4, core: 2. Of those that a mesh axis runs over, the one named last changes fastest.
Arguments:
- query_prints: bfloat16 [256, 2048], P('qry'), may hold values from -500 to 500, as said below
- library_prints: bfloat16 [24576, 2048], P(('lib', 'qry')), may hold values from -1500 to 1500
- query_atoms: float32 [256, 192], P(('qry', 'lib')), may hold values from -3 to 3, as said below
- conformer_atoms: float32 [24576, 192], P(('lib', 'qry')), may hold values from -3 to 3, as said below
- candidates: int32 [256, 64], P(('qry', 'lib')), may hold values from 0 to 24575, as said below
- candidate_count: int32 [256], P(('qry', 'lib')), may hold values from 16 to 64
- home_row: int32 [24576], replicated, may hold values from 0 to 24575, as said below
Outputs:
- tversky: bfloat16 [256, 24576], P(None, ('lib', 'qry'))
- rescore: float32 [256, 64], P(('qry', 'lib'))
The draws below stay inside these ranges and needn't reach their ends.
Inputs may be any that keep to these rules, and one draw needn't show every extreme that they name: query_prints rows and columns carry independent positive scales. `query_atoms`: each row holds x, y and z of 48 atom slots, then their weights; a padded slot has weight 0, and every row has at least one atom of positive weight. `conformer_atoms`: each row holds x, y and z of 48 atom slots, then their weights; a padded slot has weight 0, and every row has at least one atom of positive weight. Among the candidates in the rows of one device (8 queries, padding included), at most 36 have storage rows in any one block of rows b * 768 to (b + 1) * 768 - 1; in every draw some such block receives exactly 36 from the rows of every device. `home_row`: a permutation of 0 to 24575.
All inputs are finite; a program needn't handle non-finite values.
Results may differ from the reference program's by a relative error of at most 0.0029.
Values may be sent and summed in bfloat16 or wider, within the bound.
A program may use at most 64 MiB of HBM per device.

```python
import math
import jax
import jax.numpy as jnp
from jax import lax

F = 2048
ATOMS = 48
CAND = 64
QRY_DEV = 8
LIB_SH = 768
Q = 256
LIB = 24576
CAP = 36


def home_table(key):
    return jax.random.permutation(jax.random.fold_in(key, 11), LIB).astype(jnp.int32)


def draw_home_row(key, part):
    return home_table(key)


def draw_candidates(key, part):
    devices = Q // QRY_DEV
    pairs = QRY_DEV * CAND
    inverse = jnp.argsort(home_table(key), stable=True).astype(jnp.int32)
    base = jax.random.fold_in(key, 23)
    hottest = jax.random.randint(jax.random.fold_in(base, 1), (), 0, devices)
    offsets = jax.random.randint(jax.random.fold_in(base, 2), (devices, 1), 0, devices - 1)
    order = jnp.arange(pairs, dtype=jnp.int32)[None, :]
    others = (offsets + order - CAP) % (devices - 1)
    others = others + (others >= hottest).astype(jnp.int32)
    owner_by_rank = jnp.where(order < CAP, hottest, others)
    keys = jax.random.split(jax.random.fold_in(base, 3), devices)
    shuffles = jax.vmap(lambda single: jax.random.permutation(single, pairs))(keys)
    ranks = jnp.argsort(shuffles, axis=1, stable=True)
    owners = jnp.take_along_axis(owner_by_rank, ranks, axis=1)
    within = jax.random.randint(jax.random.fold_in(base, 4), (devices, pairs), 0, LIB_SH)
    stored = owners * LIB_SH + within
    return inverse[stored].reshape(Q, CAND).astype(jnp.int32)


def draw_query_prints(key, part):
    row_scale = jnp.exp(jax.random.uniform(jax.random.fold_in(key, 1), (Q, 1), minval=0.0, maxval=math.log(10.0)))
    col_scale = jnp.exp(jax.random.uniform(jax.random.fold_in(key, 2), (1, F), minval=0.0, maxval=math.log(10.0)))
    noise = jnp.clip(jax.random.normal(jax.random.fold_in(key, 3), (Q, F)), -5.0, 5.0)
    return (noise * row_scale * col_scale).astype(jnp.bfloat16)


def draw_library_prints(key, part):
    row_scale = jnp.exp(jax.random.uniform(jax.random.fold_in(key, 1), (LIB, 1), minval=math.log(100.0), maxval=math.log(300.0)))
    noise = jnp.clip(jax.random.normal(jax.random.fold_in(key, 3), (LIB, F)), -5.0, 5.0)
    return (noise * row_scale).astype(jnp.bfloat16)


def pack_atoms(key, places, weights, fewest):
    rows = places.shape[0]
    counts = jax.random.randint(jax.random.fold_in(key, 9), (rows, 1, 1), fewest, ATOMS + 1)
    live = (jnp.arange(ATOMS)[None, None, :] < counts).astype(jnp.float32)
    return jnp.concatenate([places, weights * live], axis=1).reshape(rows, 4 * ATOMS)


def draw_query_atoms(key, part):
    places = jax.random.uniform(jax.random.fold_in(key, 1), (Q, 3, ATOMS), minval=-3.0, maxval=3.0)
    weights = jax.random.uniform(jax.random.fold_in(key, 2), (Q, 1, ATOMS), minval=0.5, maxval=1.5)
    return pack_atoms(key, places, weights, max(1, ATOMS // 6))


def draw_conformer_atoms(key, part):
    places = jax.random.uniform(jax.random.fold_in(key, 1), (LIB, 3, ATOMS), minval=-3.0, maxval=3.0)
    weights = jax.random.uniform(jax.random.fold_in(key, 2), (LIB, 1, ATOMS), minval=0.5, maxval=1.5)
    return pack_atoms(key, places, weights, max(1, ATOMS // 2))


def plant(values, own_key, least, high):
    index_at = [jax.random.randint(jax.random.fold_in(own_key, axis), (), 0, length) for axis, length in enumerate(values.shape)]
    main_axis = values.shape.index(max(values.shape))
    neighbour = index_at[:main_axis] + [(index_at[main_axis] + 1) % values.shape[main_axis]] + index_at[main_axis + 1:]
    return values.at[tuple(index_at)].set(least).at[tuple(neighbour)].set(high)


def setup_inputs(seed: int = 0) -> dict:
    splits = jax.random.split(jax.random.key(seed), 8)
    query_prints = draw_query_prints(jax.random.fold_in(splits[7], 71), 0)
    library_prints = draw_library_prints(jax.random.fold_in(splits[7], 71), 0)
    query_atoms = draw_query_atoms(jax.random.fold_in(splits[7], 71), 0)
    conformer_atoms = draw_conformer_atoms(jax.random.fold_in(splits[7], 71), 0)
    candidates = draw_candidates(jax.random.fold_in(splits[7], 71), 0)
    candidate_count = plant(jax.random.randint(splits[5], (Q,), CAND // 4, CAND + 1), jax.random.fold_in(splits[5], 1), CAND // 4, CAND).astype(jnp.int32)
    home_row = draw_home_row(jax.random.fold_in(splits[7], 71), 0)
    return dict(query_prints=query_prints, library_prints=library_prints, query_atoms=query_atoms, conformer_atoms=conformer_atoms, candidates=candidates, candidate_count=candidate_count, home_row=home_row)


SHARPNESS = 0.8
EPSILON = 1e-6


def screen_rows(piece, library):
    scores = lax.dot_general(piece, library, (((1,), (1,)), ((), ())), preferred_element_type=jnp.float32)
    norms = jnp.sum(jnp.square(piece.astype(jnp.float32)), axis=1, keepdims=True)
    return (scores / (norms + EPSILON)).astype(jnp.bfloat16)


def to_atoms(flat):
    return flat.reshape(flat.shape[0], 4, -1).transpose(1, 2, 0)


def intersection(first, second):
    dist = jnp.square(first[0][:, None, :] - second[0][None, :, :])
    dist = dist + jnp.square(first[1][:, None, :] - second[1][None, :, :])
    dist = dist + jnp.square(first[2][:, None, :] - second[2][None, :, :])
    return jnp.sum(first[3][:, None, :] * second[3][None, :, :] * jnp.exp(-SHARPNESS * dist), axis=(0, 1))


def reference(query_prints, library_prints, query_atoms, conformer_atoms, candidates, candidate_count, home_row):
    blocks = query_prints.reshape(8, -1, query_prints.shape[1])
    tversky = lax.map(lambda block: screen_rows(block, library_prints), blocks).reshape(query_prints.shape[0], -1)
    stored = home_row[candidates]
    n_blocks = Q // QRY_DEV

    def rescore_block(args):
        frag_rows, block_rows, counts, block_queries = args
        flat_rows = block_rows.reshape(-1)
        conformer = to_atoms(conformer_atoms[flat_rows])
        fragment = to_atoms(jnp.repeat(frag_rows, CAND, axis=0))
        cross = intersection(fragment, conformer)
        conformer_self = intersection(conformer, conformer)
        frag_atoms = to_atoms(frag_rows)
        query_self = jnp.repeat(intersection(frag_atoms, frag_atoms), CAND)
        prior = tversky[jnp.repeat(block_queries, CAND), flat_rows].astype(jnp.float32)
        shape = cross / (query_self + conformer_self - cross)
        live = jnp.arange(CAND, dtype=jnp.int32)[None, :] < counts[:, None]
        return jnp.where(live, (shape + prior).reshape(-1, CAND), 0.0)

    result = lax.map(rescore_block, (query_atoms.reshape(n_blocks, QRY_DEV, -1), stored.reshape(n_blocks, QRY_DEV, CAND), candidate_count.reshape(n_blocks, QRY_DEV), jnp.arange(Q, dtype=jnp.int32).reshape(n_blocks, QRY_DEV)))
    return tversky, result.reshape(Q, CAND)
```

```python
import functools
import math

import jax
import jax.numpy as jnp
from jax import lax
from jax.experimental import pallas as pl
from jax.experimental.pallas import tpu as pltpu
from jax.sharding import PartitionSpec as P

SHARPNESS = 0.8
EPSILON = 1e-06
LANES = 128
CORES = 2
SCALE = SHARPNESS * math.log2(math.e)
ROOT = math.sqrt(2.0 * SCALE)

F32 = jnp.float32
BF16 = jnp.bfloat16
I32 = jnp.int32


def nt(a, b):
    return lax.dot_general(a, b, (((1,), (1,)), ((), ())), preferred_element_type=F32)


def nn(a, b):
    return lax.dot_general(a, b, (((1,), (0,)), ((), ())), preferred_element_type=F32)


def split2(x):
    hi = x.astype(BF16)
    return hi, (x - hi.astype(F32)).astype(BF16)


def iota(shape, dim):
    return lax.broadcasted_iota(I32, shape, dim)


def fdiv(x, by):
    return jnp.floor((x.astype(F32) + 0.5) * (1.0 / by)).astype(I32)


def prepare(x, y, z, w):
    norm = SCALE * (x * x + y * y + z * z)
    return x * ROOT, y * ROOT, z * ROOT, w * jnp.exp2(-norm)


def self_overlap(ref, lanes, atoms):
    blocks = atoms // 8
    comp = [[ref[pl.ds(c * atoms + 8 * i, 8), lanes] for i in range(blocks)] for c in range(4)]
    total = None
    diag = [None] * blocks
    off = [None] * blocks
    for a in range(atoms):
        xa, ya, za, wa = (ref[pl.ds(c * atoms + a, 1), lanes] for c in range(4))
        wa2 = wa + wa
        for i in range(a // 8, blocks):
            e = jnp.exp2(xa * comp[0][i] + ya * comp[1][i] + za * comp[2][i])
            if i == a // 8:
                diag[i] = wa * e if diag[i] is None else diag[i] + wa * e
            else:
                off[i] = wa2 * e if off[i] is None else off[i] + wa2 * e
    for i in range(blocks):
        part = diag[i] if off[i] is None else diag[i] + off[i]
        part = part * comp[3][i]
        total = part if total is None else total + part
    return jnp.sum(total, axis=0, keepdims=True)


def cross_overlap(qref, cref, lanes, atoms):
    comp = [cref[pl.ds(c * atoms, atoms), lanes] for c in range(4)]
    acc = None
    for a in range(atoms):
        xa, ya, za, wa = (qref[pl.ds(c * atoms + a, 1), lanes] for c in range(4))
        e = wa * jnp.exp2(xa * comp[0] + ya * comp[1] + za * comp[2])
        acc = e if acc is None else acc + e
    return jnp.sum(acc * comp[3], axis=0, keepdims=True)


def flip(x, bits):
    step, out = 1, x
    while step < 256:
        one = lax.rem(lax.div(x, step), 2)
        other = lax.rem(lax.div(bits, step), 2) if not isinstance(bits, int) else (bits // step) % 2
        out = out + other * (1 - 2 * one) * step
        step *= 2
        if isinstance(bits, int) and step > bits:
            break
    return out


def kernel(
    nq, nl, cap, id_bytes,
    qp_hbm, lib_hbm, qa_hbm, conf_hbm, cand_hbm, count_hbm, home_hbm,
    tv_hbm, out_ref,
    tv_ref,
    qp_ref, qa_ref, cand_ref, count_ref, home_ref,
    lib, conf, gath, pack, atoms_in, codes_out, codes_in, score, ret_in,
    confp, qprep, ownprep, pairs_c, pairs_q, onehot, qonehot, cself, shape_s,
    loc_sem, s1_send, s1_recv, sib_send, sib_recv, s2_send, s2_recv,
    send_a, recv_a, send_b, recv_b, send_c, recv_c, send_d, recv_d,
):
    q = lax.axis_index("qry")
    l = lax.axis_index("lib")
    dev = nq * nl
    me = q * nl + l
    me_o = l * nq + q
    nz = nq // CORES
    z, c = lax.div(q, CORES), lax.rem(q, CORES)
    sib = z * CORES + (1 - c)
    own_rows = lib.shape[0]
    block = qp_ref.shape[0]
    cols = gath.shape[2]
    local_q, listed = cand_ref.shape
    cand_n = local_q * listed
    atoms = qa_ref.shape[1] // 4
    half = 2 * atoms
    pairs = onehot.shape[1]
    groups = pairs // LANES

    spread = [(d, e) for d in range(nq) for e in range(nl) if d or e]
    spread.sort(key=lambda o: -(o[0] // CORES + bin(o[1]).count("1")))
    peers = [(flip(q, d) if d else q, flip(l, e) if e else l) for d, e in spread]
    lib_peers = [flip(l, e) for e in range(1, nl)]
    qry_peers = [flip(q, d) for d in range(nq - 1, 0, -1)]

    def take(ref, sem):
        pltpu.make_async_copy(ref, ref, sem).wait()

    def remote(src, dst, ssem, rsem, dq, dl):
        return pltpu.make_async_remote_copy(
            src_ref=src, dst_ref=dst, send_sem=ssem, recv_sem=rsem,
            device_id={"qry": dq, "lib": dl}, device_id_type=pl.DeviceIdType.MESH,
        )

    barrier = pltpu.get_barrier_semaphore()
    loads = [
        pltpu.make_async_copy(src, dst, loc_sem.at[2 + n])
        for n, (src, dst) in enumerate(
            ((qa_hbm, qa_ref), (cand_hbm, cand_ref), (home_hbm, home_ref), (qp_hbm, qp_ref), (count_hbm, count_ref))
        )
    ]
    for load in loads:
        load.start()
    lib_copy = pltpu.make_async_copy(lib_hbm, lib, loc_sem.at[0])
    conf_copy = pltpu.make_async_copy(conf_hbm, conf, loc_sem.at[1])
    conf_copy.start()
    lib_copy.start()

    for tq, tl in peers:
        pl.semaphore_signal(
            barrier, inc=1, device_id={"qry": tq, "lib": tl}, device_id_type=pl.DeviceIdType.MESH
        )

    for load in loads:
        load.wait()

    ids = jnp.concatenate([cand_ref[pl.ds(i, 1), :] for i in range(local_q)], axis=1)
    table = home_ref[...]
    trows = table.shape[0]
    pieces = [
        jnp.transpose(((table >> (8 * k)) & 255).astype(F32)).astype(BF16) for k in range(id_bytes)
    ]
    row_hot = jnp.where(iota((trows, cand_n), 0) == (ids >> 7), 1.0, 0.0).astype(BF16)
    lane_hot = iota((LANES, cand_n), 0) == (ids & 127)
    stored = jnp.zeros((1, cand_n), I32)
    for k in range(id_bytes):
        found = nn(pieces[k], row_hot)
        byte = jnp.sum(jnp.where(lane_hot, found, 0.0), axis=0, keepdims=True)
        stored = stored + (byte.astype(I32) << (8 * k))
    owner = fdiv(stored, own_rows)
    slot = stored - owner * own_rows

    owns = iota((dev, cand_n), 0) == owner
    owns_b = jnp.where(owns, 1.0, 0.0).astype(BF16)
    tri = jnp.where(iota((cand_n, cand_n), 0) < iota((cand_n, cand_n), 1), 1.0, 0.0).astype(BF16)
    before = nn(owns_b, tri)
    rank = jnp.sum(jnp.where(owns, before, 0.0), axis=0, keepdims=True).astype(I32)
    my_off = lax.rem(cap * me, LANES)
    rank_b = jnp.where(iota((2 * LANES, cand_n), 0) == rank + my_off, 1.0, 0.0).astype(BF16)
    code = slot * local_q + fdiv(iota((1, cand_n), 1), listed) + 1
    lo = (code & 127).astype(F32)
    hi = (code >> 7).astype(F32)
    left = jnp.concatenate([jnp.where(owns, lo, 0.0), jnp.where(owns, hi, 0.0)], axis=0).astype(BF16)
    sums = nt(left, rank_b).astype(I32)
    codes = sums[:dev] + (sums[dev:] << 7)
    for o in range(dev):
        for k in range(2):
            codes_out[o, k] = codes[o : o + 1, k * LANES : (k + 1) * LANES]

    qa = qa_ref[...]
    zero = jnp.zeros((local_q, LANES - half), F32)
    top = jnp.concatenate([qa[:, :half], zero], axis=1)
    low = jnp.concatenate([qa[:, half:], zero], axis=1)
    fill = jnp.zeros((LANES - local_q, LANES), F32)
    top_t = jnp.transpose(jnp.concatenate([top, fill], axis=0))
    low_t = jnp.transpose(jnp.concatenate([low, fill], axis=0))
    comps = prepare(top_t[:atoms], top_t[atoms:half], low_t[:atoms], low_t[atoms:half])
    for i in range(4):
        ownprep[i * atoms : (i + 1) * atoms] = comps[i]
    own_self = self_overlap(ownprep, pl.ds(0, LANES), atoms)
    lane_at = iota((local_q, LANES), 1)
    own_col = jnp.sum(
        jnp.where(lane_at == iota((local_q, LANES), 0), own_self, 0.0), axis=1, keepdims=True
    )
    own_hi = own_col.astype(BF16).astype(F32)
    low = jnp.where(lane_at == half, own_hi, jnp.where(lane_at == half + 1, own_col - own_hi, low))
    pack[...] = jnp.concatenate([top, low], axis=0).astype(BF16)

    pl.semaphore_wait(barrier, dev - 1)

    def piece(bq, k):
        return gath.at[k, pl.ds(pl.multiple_of(bq * block, block), block), :]

    def from_z(d):
        return flip(z, d) * CORES + c

    def stage1(d):
        return remote(
            qp_ref.at[:, pl.ds(pl.multiple_of(l * cols, cols), cols)], piece(q, l),
            s1_send, s1_recv.at[d], from_z(d), l,
        )

    def stage2(d, e):
        there = piece(from_z(d), l)
        return remote(there, there, s2_send, s2_recv.at[d, e], q, flip(l, e))

    def to_sib(bq, k):
        there = piece(bq, k)
        return remote(there, there, sib_send, sib_recv, sib, l)

    for d in range(1, nz):
        stage1(d).start()
    for t in qry_peers:
        remote(pack, atoms_in.at[q, l], send_a, recv_a, t, l).start()
    for tq, tl in peers:
        remote(codes_out.at[tl * nq + tq], codes_in.at[me], send_c, recv_c, tq, tl).start()
    for k in range(nl):
        gath[k, pl.ds(pl.multiple_of(q * block, block), block), :] = qp_ref[:, k * cols : (k + 1) * cols]
    for k in range(nl):
        to_sib(q, k).start()
    atoms_in[q, l] = pack[...]
    codes_in[me] = codes_out[me_o]

    conf_copy.wait()
    comps = prepare(*(conf[i * atoms : (i + 1) * atoms] for i in range(4)))
    for i in range(4):
        confp[i * atoms : (i + 1) * atoms] = comps[i]

    def self_step(g, carry):
        lanes = pl.ds(pl.multiple_of(g * LANES, LANES), LANES)
        cself[0:1, lanes] = self_overlap(confp, lanes, atoms)
        return carry

    lax.fori_loop(0, own_rows // LANES, self_step, 0)

    q_rest = pl.ds(0, nq - 1)
    l_rest = pl.ds(0, nl - 1)
    d_rest = pl.ds(0, dev - 1)

    for d in range(1, nz):
        stage1(d).wait_recv()
        for e in range(nl - 1, 0, -1):
            stage2(d, e).start()
        to_sib(from_z(d), l).start()
        if d == 1:
            take(atoms_in.at[q_rest, 0], recv_a)
            for t in lib_peers:
                remote(atoms_in.at[:, l], atoms_in.at[:, l], send_b, recv_b, q, t).start()

    take(codes_in.at[d_rest], recv_c)
    parts = [None] * groups
    for s in range(dev):
        g = cap * s // LANES
        for k in range(2):
            if g + k < groups:
                row = codes_in[s, k]
                parts[g + k] = row if parts[g + k] is None else parts[g + k] + row
    none = jnp.zeros((1, LANES), I32)
    pcode = jnp.concatenate([none if p is None else p for p in parts], axis=1)
    valid = pcode > 0
    pcode = jnp.maximum(pcode - 1, 0)
    pslot = fdiv(pcode, local_q)
    pquery = fdiv(iota((1, pairs), 1), cap) * local_q + (pcode - pslot * local_q)
    onehot[...] = jnp.where(iota((own_rows, pairs), 0) == pslot, 1.0, 0.0).astype(BF16)
    qonehot[...] = jnp.where(iota((dev * local_q, pairs), 0) == pquery, 1.0, 0.0).astype(BF16)

    pad = jnp.zeros((7, own_rows), F32)
    hi_c, lo_c = split2(jnp.concatenate([confp[...], cself[...], pad], axis=0))
    pairs_c[...] = nn(hi_c, onehot[...]) + nn(lo_c, onehot[...])

    take(atoms_in.at[:, l_rest], recv_b)
    raw = atoms_in[...].reshape(dev, 2 * local_q, LANES).astype(F32)
    q_top = jnp.transpose(raw[:, :local_q].reshape(dev * local_q, LANES))
    q_low = jnp.transpose(raw[:, local_q:].reshape(dev * local_q, LANES))
    comps = prepare(q_top[:atoms], q_top[atoms:half], q_low[:atoms], q_low[atoms:half])
    for i in range(4):
        qprep[i * atoms : (i + 1) * atoms] = comps[i]
    qself = q_low[half : half + 1] + q_low[half + 1 : half + 2]
    pad = jnp.zeros((7, dev * local_q), F32)
    hi_q, lo_q = split2(jnp.concatenate([qprep[...], qself, pad], axis=0))
    pairs_q[...] = nn(hi_q, qonehot[...]) + nn(lo_q, qonehot[...])

    n_far = (nz - 1) * (nl - 1)
    each = (n_far + groups - 1) // groups

    def onward(n):
        d = 1 + lax.div(n, nl - 1)
        e = nl - 1 - lax.rem(n, nl - 1)
        stage2(d, e).wait_recv()
        to_sib(from_z(d), flip(l, e)).start()

    def cross_step(g, carry):
        for k in range(each):
            n = g * each + k
            if groups * each == n_far:
                onward(n)
            else:
                pl.when(n < n_far)(functools.partial(onward, n))
        lanes = pl.ds(pl.multiple_of(g * LANES, LANES), LANES)
        cross = cross_overlap(pairs_q, pairs_c, lanes, atoms)
        selves = pairs_q[4 * atoms : 4 * atoms + 1, lanes] + pairs_c[4 * atoms : 4 * atoms + 1, lanes]
        shape_s[0:1, lanes] = cross / (selves - cross)
        return carry

    lax.fori_loop(0, groups, cross_step, 0)

    take(gath.at[:, pl.ds(0, nz * block), :], sib_recv)
    lib_copy.wait()

    rows = nq * block
    chunk = min(rows, 256)
    for r in range(0, rows, chunk):
        scores = None
        norms = None
        for k in range(nl):
            part = gath[k, r : r + chunk, :]
            prod = nt(part, lib[:, k * cols : (k + 1) * cols])
            wide = part.astype(F32)
            sq = jnp.sum(wide * wide, axis=1, keepdims=True)
            scores = prod if scores is None else scores + prod
            norms = sq if norms is None else norms + sq
        tv_ref[r : r + chunk, :] = (scores * (1.0 / (norms + EPSILON))).astype(BF16)

    tv_copy = pltpu.make_async_copy(tv_ref, tv_hbm, loc_sem.at[7])
    tv_copy.start()
    for g in range(groups):
        first = LANES * g // cap * local_q // 16 * 16
        last = min((LANES * g + LANES - 1) // cap * local_q // 16 * 16 + 16, rows)
        lanes = slice(g * LANES, (g + 1) * LANES)
        chosen = nn(tv_ref[first:last, :], onehot[:, lanes])
        mine = iota((last - first, LANES), 0) + first == pquery[:, lanes]
        prior = jnp.sum(jnp.where(mine, chosen, 0.0), axis=0, keepdims=True)
        score[g] = jnp.where(valid[:, lanes], shape_s[:, lanes] + prior, 0.0)
    score[groups] = jnp.zeros((1, LANES), F32)

    for tq, tl in peers:
        at = lax.div(cap * (tq * nl + tl), LANES)
        remote(score.at[pl.ds(at, 2)], ret_in.at[me_o], send_d, recv_d, tq, tl).start()
    ret_in[me_o] = score[pl.ds(lax.div(cap * me, LANES), 2)]

    take(gath.at[0, pl.ds(0, (nz - 1) * block), :], s1_send)
    take(gath.at[pl.ds(0, nl - 1), pl.ds(0, (nz - 1) * block), :], s2_send)
    take(gath.at[:, pl.ds(0, nz * block), :], sib_send)
    take(atoms_in.at[q_rest, 0], send_a)
    take(atoms_in.at[:, l_rest], send_b)
    take(codes_in.at[d_rest], send_c)
    tv_copy.wait()
    take(ret_in.at[d_rest], recv_d)

    came = jnp.concatenate([ret_in[:, k].reshape(dev, LANES) for k in range(2)], axis=1)
    hi_b, lo_b = split2(came)
    mine = nn(hi_b, rank_b) + nn(lo_b, rank_b)
    final = jnp.sum(jnp.where(owns, mine, 0.0), axis=0, keepdims=True)
    for i in range(local_q):
        line = final[:, i * listed : (i + 1) * listed]
        live = iota((1, listed), 1) < count_ref[i]
        out_ref[i : i + 1, :] = jnp.where(live, line, 0.0)

    take(ret_in.at[d_rest], send_d)


def copy_out(tv_in, score_in, tv_out, score_out, sems):
    copies = [
        pltpu.make_async_copy(tv_in, tv_out, sems.at[0]),
        pltpu.make_async_copy(score_in, score_out, sems.at[1]),
    ]
    for copy in copies:
        copy.start()
    for copy in copies:
        copy.wait()


def hand_over(tv, score):
    return pl.pallas_call(
        copy_out,
        out_shape=(jax.ShapeDtypeStruct(tv.shape, tv.dtype), jax.ShapeDtypeStruct(score.shape, score.dtype)),
        in_specs=[pl.BlockSpec(memory_space=pltpu.VMEM)] * 2,
        out_specs=(pl.BlockSpec(memory_space=pl.ANY), pl.BlockSpec(memory_space=pl.ANY)),
        scratch_shapes=[pltpu.SemaphoreType.DMA((2,))],
    )(tv, score)


def body(nq, nl, query_prints, library_prints, query_atoms, conformer_atoms, candidates, candidate_count, home_row):
    dev = nq * nl
    block, width = query_prints.shape
    own_rows = library_prints.shape[0]
    local_q, listed = candidates.shape
    atoms = query_atoms.shape[1] // 4
    cand_n = local_q * listed
    cap = 2 * ((cand_n + dev - 1) // dev) + 4
    pairs = (dev * cap + LANES - 1) // LANES * LANES
    id_bytes = ((home_row.shape[0] - 1).bit_length() + 7) // 8
    rows = nq * block
    nz = nq // CORES
    limit = 56 * 1024 * 1024
    vm = pltpu.VMEM
    dma = pltpu.SemaphoreType.DMA
    vspec = pl.BlockSpec(memory_space=pltpu.VMEM)
    tv, score = pl.pallas_call(
        functools.partial(kernel, nq, nl, cap, id_bytes),
        out_shape=(
            jax.ShapeDtypeStruct((rows, own_rows), BF16),
            jax.ShapeDtypeStruct((local_q, listed), F32),
        ),
        in_specs=[pl.BlockSpec(memory_space=pltpu.HBM)] * 7,
        out_specs=(pl.BlockSpec(memory_space=pl.ANY), vspec),
        scratch_shapes=[
            vm((rows, own_rows), BF16),
            vm((block, width), BF16),
            vm((local_q, 4 * atoms), F32),
            vm((local_q, listed), I32),
            pltpu.SMEM((local_q,), I32),
            vm((home_row.shape[0] // LANES, LANES), I32),
            vm((own_rows, width), BF16),
            vm((4 * atoms, own_rows), F32),
            vm((nl, rows, width // nl), BF16),
            vm((2 * local_q, LANES), BF16),
            vm((nq, nl, 2 * local_q, LANES), BF16),
            vm((dev, 2, 1, LANES), I32),
            vm((dev, 2, 1, LANES), I32),
            vm((pairs // LANES + 1, 1, LANES), F32),
            vm((dev, 2, 1, LANES), F32),
            vm((4 * atoms, own_rows), F32),
            vm((4 * atoms, rows), F32),
            vm((4 * atoms, LANES), F32),
            vm((4 * atoms + 8, pairs), F32),
            vm((4 * atoms + 8, pairs), F32),
            vm((own_rows, pairs), BF16),
            vm((rows, pairs), BF16),
            vm((1, own_rows), F32),
            vm((1, pairs), F32),
            dma((8,)),
            dma, dma((nz,)),
            dma, dma,
            dma, dma((nz, nl)),
            dma, dma, dma, dma, dma, dma, dma, dma,
        ],
        compiler_params=pltpu.CompilerParams(
            collective_id=0, has_side_effects=True, vmem_limit_bytes=limit
        ),
    )(
        query_prints, library_prints, query_atoms, conformer_atoms.T, candidates, candidate_count,
        home_row.reshape(-1, LANES),
    )
    return hand_over(tv, score)


def solution(mesh):
    return jax.shard_map(
        functools.partial(body, mesh.shape["qry"], mesh.shape["lib"]),
        mesh=mesh,
        in_specs=(
            P("qry", None),
            P(("lib", "qry"), None),
            P(("qry", "lib"), None),
            P(("lib", "qry"), None),
            P(("qry", "lib"), None),
            P(("qry", "lib")),
            P(),
        ),
        out_specs=(P(None, ("lib", "qry")), P(("qry", "lib"), None)),
        check_vma=False,
    )
```

```python
import functools
import math

import jax
import jax.numpy as jnp
from jax import lax
from jax.experimental import pallas as pl
from jax.experimental.pallas import tpu as pltpu
from jax.sharding import PartitionSpec as P

SHARPNESS = 0.8
EPSILON = 1e-06
LANES = 128
CORES = 2
SCALE = SHARPNESS * math.log2(math.e)
ROOT = math.sqrt(2.0 * SCALE)

F32 = jnp.float32
BF16 = jnp.bfloat16
I32 = jnp.int32


def nt(a, b):
    return lax.dot_general(a, b, (((1,), (1,)), ((), ())), preferred_element_type=F32)


def nn(a, b):
    return lax.dot_general(a, b, (((1,), (0,)), ((), ())), preferred_element_type=F32)


def split2(x):
    hi = x.astype(BF16)
    return hi, (x - hi.astype(F32)).astype(BF16)


def iota(shape, dim):
    return lax.broadcasted_iota(I32, shape, dim)


def fdiv(x, by):
    return jnp.floor((x.astype(F32) + 0.5) * (1.0 / by)).astype(I32)


def prepare(x, y, z, w):
    norm = SCALE * (x * x + y * y + z * z)
    return x * ROOT, y * ROOT, z * ROOT, w * jnp.exp2(-norm)


def self_overlap(ref, lanes, atoms):
    blocks = atoms // 8
    comp = [[ref[pl.ds(c * atoms + 8 * i, 8), lanes] for i in range(blocks)] for c in range(4)]
    total = None
    diag = [None] * blocks
    off = [None] * blocks
    for a in range(atoms):
        xa, ya, za, wa = (ref[pl.ds(c * atoms + a, 1), lanes] for c in range(4))
        wa2 = wa + wa
        for i in range(a // 8, blocks):
            e = jnp.exp2(xa * comp[0][i] + ya * comp[1][i] + za * comp[2][i])
            if i == a // 8:
                diag[i] = wa * e if diag[i] is None else diag[i] + wa * e
            else:
                off[i] = wa2 * e if off[i] is None else off[i] + wa2 * e
    for i in range(blocks):
        part = diag[i] if off[i] is None else diag[i] + off[i]
        part = part * comp[3][i]
        total = part if total is None else total + part
    return jnp.sum(total, axis=0, keepdims=True)


def cross_overlap(qref, cref, lanes, atoms):
    comp = [cref[pl.ds(c * atoms, atoms), lanes] for c in range(4)]
    acc = None
    for a in range(atoms):
        xa, ya, za, wa = (qref[pl.ds(c * atoms + a, 1), lanes] for c in range(4))
        e = wa * jnp.exp2(xa * comp[0] + ya * comp[1] + za * comp[2])
        acc = e if acc is None else acc + e
    return jnp.sum(acc * comp[3], axis=0, keepdims=True)


def flip(x, bits):
    step, out = 1, x
    while step < 256:
        one = lax.rem(lax.div(x, step), 2)
        other = lax.rem(lax.div(bits, step), 2) if not isinstance(bits, int) else (bits // step) % 2
        out = out + other * (1 - 2 * one) * step
        step *= 2
        if isinstance(bits, int) and step > bits:
            break
    return out


def kernel(
    nq, nl, cap, id_bytes,
    qp_hbm, lib_hbm, qa_hbm, conf_hbm, cand_hbm, count_hbm, home_hbm,
    tv_hbm, out_ref,
    tv_ref,
    qp_ref, qa_ref, cand_ref, count_ref, home_ref,
    lib, conf, gath, pack, atoms_in, codes_out, codes_in, score, ret_in,
    confp, qprep, ownprep, pairs_c, pairs_q, onehot, qonehot, cself, shape_s,
    loc_sem, s1_send, s1_recv, sib_send, sib_recv, s2_send, s2_recv,
    send_a, recv_a, send_b, recv_b, send_c, recv_c, send_d, recv_d, send_e, recv_e, ready,
):
    q = lax.axis_index("qry")
    l = lax.axis_index("lib")
    dev = nq * nl
    me = q * nl + l
    me_o = l * nq + q
    nz = nq // CORES
    z, c = lax.div(q, CORES), lax.rem(q, CORES)
    sib = z * CORES + (1 - c)
    own_rows = lib.shape[0]
    block = qp_ref.shape[0]
    cols = gath.shape[2]
    local_q, listed = cand_ref.shape
    cand_n = local_q * listed
    atoms = qa_ref.shape[1] // 4
    half = 2 * atoms
    pairs = onehot.shape[1]
    groups = pairs // LANES

    spread = [(d, e) for d in range(nq) for e in range(nl) if d or e]
    spread.sort(key=lambda o: -(o[0] // CORES + bin(o[1]).count("1")))
    near = [(q, flip(l, e)) for e in range(nl - 1, 0, -1)] + [(flip(q, d), l) for d in range(nq - 1, 0, -1)]
    peers = [(flip(q, d) if d else q, flip(l, e) if e else l) for d, e in spread]

    def take(ref, sem):
        pltpu.make_async_copy(ref, ref, sem).wait()

    def remote(src, dst, ssem, rsem, dq, dl):
        return pltpu.make_async_remote_copy(
            src_ref=src, dst_ref=dst, send_sem=ssem, recv_sem=rsem,
            device_id={"qry": dq, "lib": dl}, device_id_type=pl.DeviceIdType.MESH,
        )

    barrier = pltpu.get_barrier_semaphore()
    loads = [
        pltpu.make_async_copy(src, dst, loc_sem.at[2 + n])
        for n, (src, dst) in enumerate(
            ((qa_hbm, qa_ref), (cand_hbm, cand_ref), (home_hbm, home_ref), (qp_hbm, qp_ref), (count_hbm, count_ref))
        )
    ]
    for load in loads:
        load.start()
    lib_copy = pltpu.make_async_copy(lib_hbm, lib, loc_sem.at[0])
    conf_copy = pltpu.make_async_copy(conf_hbm, conf, loc_sem.at[1])
    conf_copy.start()
    lib_copy.start()

    for tq, tl in near:
        pl.semaphore_signal(
            barrier, inc=1, device_id={"qry": tq, "lib": tl}, device_id_type=pl.DeviceIdType.MESH
        )

    for load in loads:
        load.wait()

    ids = jnp.concatenate([cand_ref[pl.ds(i, 1), :] for i in range(local_q)], axis=1)
    table = home_ref[...]
    trows = table.shape[0]
    pieces = [
        jnp.transpose(((table >> (8 * k)) & 255).astype(F32)).astype(BF16) for k in range(id_bytes)
    ]
    row_hot = jnp.where(iota((trows, cand_n), 0) == (ids >> 7), 1.0, 0.0).astype(BF16)
    lane_hot = iota((LANES, cand_n), 0) == (ids & 127)
    stored = jnp.zeros((1, cand_n), I32)
    for k in range(id_bytes):
        found = nn(pieces[k], row_hot)
        byte = jnp.sum(jnp.where(lane_hot, found, 0.0), axis=0, keepdims=True)
        stored = stored + (byte.astype(I32) << (8 * k))
    owner = fdiv(stored, own_rows)
    slot = stored - owner * own_rows

    owns = iota((dev, cand_n), 0) == owner
    owns_b = jnp.where(owns, 1.0, 0.0).astype(BF16)
    tri = jnp.where(iota((cand_n, cand_n), 0) < iota((cand_n, cand_n), 1), 1.0, 0.0).astype(BF16)
    before = nn(owns_b, tri)
    rank = jnp.sum(jnp.where(owns, before, 0.0), axis=0, keepdims=True).astype(I32)
    my_off = lax.rem(cap * me, LANES)
    rank_b = jnp.where(iota((2 * LANES, cand_n), 0) == rank + my_off, 1.0, 0.0).astype(BF16)
    code = slot * local_q + fdiv(iota((1, cand_n), 1), listed) + 1
    lo = (code & 127).astype(F32)
    hi = (code >> 7).astype(F32)
    left = jnp.concatenate([jnp.where(owns, lo, 0.0), jnp.where(owns, hi, 0.0)], axis=0).astype(BF16)
    sums = nt(left, rank_b).astype(I32)
    codes = sums[:dev] + (sums[dev:] << 7)
    for o in range(dev):
        for k in range(2):
            codes_out[o, k] = codes[o : o + 1, k * LANES : (k + 1) * LANES]

    qa = qa_ref[...]
    zero = jnp.zeros((local_q, LANES - half), F32)
    top = jnp.concatenate([qa[:, :half], zero], axis=1)
    low = jnp.concatenate([qa[:, half:], zero], axis=1)
    fill = jnp.zeros((LANES - local_q, LANES), F32)
    top_t = jnp.transpose(jnp.concatenate([top, fill], axis=0))
    low_t = jnp.transpose(jnp.concatenate([low, fill], axis=0))
    comps = prepare(top_t[:atoms], top_t[atoms:half], low_t[:atoms], low_t[atoms:half])
    for i in range(4):
        ownprep[i * atoms : (i + 1) * atoms] = comps[i]
    own_self = self_overlap(ownprep, pl.ds(0, LANES), atoms)
    lane_at = iota((local_q, LANES), 1)
    own_col = jnp.sum(
        jnp.where(lane_at == iota((local_q, LANES), 0), own_self, 0.0), axis=1, keepdims=True
    )
    own_hi = own_col.astype(BF16).astype(F32)
    low = jnp.where(lane_at == half, own_hi, jnp.where(lane_at == half + 1, own_col - own_hi, low))
    pack[...] = jnp.concatenate([top, low], axis=0).astype(BF16)

    pl.semaphore_wait(barrier, nq + nl - 2)
    for e in range(nl - 1, 0, -1):
        pl.semaphore_signal(
            ready, inc=1, device_id={"qry": q, "lib": flip(l, e)}, device_id_type=pl.DeviceIdType.MESH
        )

    def piece(bq, k):
        return gath.at[k, pl.ds(pl.multiple_of(bq * block, block), block), :]

    def from_z(d):
        return flip(z, d) * CORES + c

    def stage1(d):
        return remote(
            qp_ref.at[:, pl.ds(pl.multiple_of(l * cols, cols), cols)], piece(q, l),
            s1_send, s1_recv.at[d], from_z(d), l,
        )

    def stage2(d, e):
        there = piece(from_z(d), l)
        return remote(there, there, s2_send, s2_recv.at[d, e], q, flip(l, e))

    def to_sib(bq, k):
        there = piece(bq, k)
        return remote(there, there, sib_send, sib_recv, sib, l)

    def atoms_to(k, dq, dl, ssem, rsem):
        there = atoms_in.at[k, c]
        return remote(there, there, ssem, rsem, dq, dl)

    for d in range(nz - 1, 0, -1):
        remote(pack, atoms_in.at[l, c, z], send_a, recv_a, from_z(d), l).start()
    for d in range(1, nz):
        stage1(d).start()
    for k in range(nl):
        gath[k, pl.ds(pl.multiple_of(q * block, block), block), :] = qp_ref[:, k * cols : (k + 1) * cols]
    for k in range(nl):
        to_sib(q, k).start()
    atoms_in[l, c, z] = pack[...]

    conf_copy.wait()
    comps = prepare(*(conf[i * atoms : (i + 1) * atoms] for i in range(4)))
    for i in range(4):
        confp[i * atoms : (i + 1) * atoms] = comps[i]

    def self_step(g, carry):
        lanes = pl.ds(pl.multiple_of(g * LANES, LANES), LANES)
        cself[0:1, lanes] = self_overlap(confp, lanes, atoms)
        return carry

    selves = own_rows // LANES
    lax.fori_loop(0, selves // 3, self_step, 0)

    pl.semaphore_wait(ready, nl - 1)
    for tq, tl in peers:
        remote(codes_out.at[tl * nq + tq], codes_in.at[me], send_c, recv_c, tq, tl).start()
    codes_in[me] = codes_out[me_o]

    lax.fori_loop(selves // 3, selves, self_step, 0)

    z_rest = pl.ds(0, nz - 1)
    l_rest = pl.ds(0, nl - 1)
    d_rest = pl.ds(0, dev - 1)

    take(atoms_in.at[0, 0, z_rest], recv_a)
    for e in range(nl - 1, 0, -1):
        atoms_to(l, q, flip(l, e), send_b, recv_b).start()
    atoms_to(l, sib, l, send_e, recv_e).start()
    for d in range(1, nz):
        stage1(d).wait_recv()
        for e in range(nl - 1, 0, -1):
            stage2(d, e).start()
        to_sib(from_z(d), l).start()

    take(codes_in.at[d_rest], recv_c)
    parts = [None] * groups
    for s in range(dev):
        g = cap * s // LANES
        for k in range(2):
            if g + k < groups:
                row = codes_in[s, k]
                parts[g + k] = row if parts[g + k] is None else parts[g + k] + row
    none = jnp.zeros((1, LANES), I32)
    pcode = jnp.concatenate([none if p is None else p for p in parts], axis=1)
    valid = pcode > 0
    pcode = jnp.maximum(pcode - 1, 0)
    pslot = fdiv(pcode, local_q)
    source = fdiv(iota((1, pairs), 1), cap)
    which = pcode - pslot * local_q
    pquery = source * local_q + which
    src_q, src_l = source // nl, source % nl
    held = ((src_l * CORES + src_q % CORES) * nz + src_q // CORES) * local_q + which
    onehot[...] = jnp.where(iota((own_rows, pairs), 0) == pslot, 1.0, 0.0).astype(BF16)
    qonehot[...] = jnp.where(iota((dev * local_q, pairs), 0) == held, 1.0, 0.0).astype(BF16)

    take(atoms_in.at[l_rest, 0], recv_b)
    for e in range(nl - 1, 0, -1):
        atoms_to(flip(l, e), sib, l, send_e, recv_e).start()

    pad = jnp.zeros((7, own_rows), F32)
    hi_c, lo_c = split2(jnp.concatenate([confp[...], cself[...], pad], axis=0))
    pairs_c[...] = nn(hi_c, onehot[...]) + nn(lo_c, onehot[...])

    take(atoms_in.at[:, 0], recv_e)
    raw = atoms_in[...].reshape(dev, 2 * local_q, LANES).astype(F32)
    q_top = jnp.transpose(raw[:, :local_q].reshape(dev * local_q, LANES))
    q_low = jnp.transpose(raw[:, local_q:].reshape(dev * local_q, LANES))
    comps = prepare(q_top[:atoms], q_top[atoms:half], q_low[:atoms], q_low[atoms:half])
    for i in range(4):
        qprep[i * atoms : (i + 1) * atoms] = comps[i]
    qself = q_low[half : half + 1] + q_low[half + 1 : half + 2]
    pad = jnp.zeros((7, dev * local_q), F32)
    hi_q, lo_q = split2(jnp.concatenate([qprep[...], qself, pad], axis=0))
    pairs_q[...] = nn(hi_q, qonehot[...]) + nn(lo_q, qonehot[...])

    n_far = (nz - 1) * (nl - 1)
    each = (2 * n_far + groups - 1) // groups

    def onward(n):
        d = 1 + lax.div(n, nl - 1)
        e = nl - 1 - lax.rem(n, nl - 1)
        stage2(d, e).wait_recv()
        to_sib(from_z(d), flip(l, e)).start()

    def cross_step(g, carry):
        for k in range(each):
            n = g * each + k
            if groups * each == n_far:
                onward(n)
            else:
                pl.when(n < n_far)(functools.partial(onward, n))
        lanes = pl.ds(pl.multiple_of(g * LANES, LANES), LANES)
        cross = cross_overlap(pairs_q, pairs_c, lanes, atoms)
        selves = pairs_q[4 * atoms : 4 * atoms + 1, lanes] + pairs_c[4 * atoms : 4 * atoms + 1, lanes]
        shape_s[0:1, lanes] = cross / (selves - cross)
        return carry

    lax.fori_loop(0, groups, cross_step, 0)

    take(gath.at[:, pl.ds(0, nz * block), :], sib_recv)
    lib_copy.wait()

    rows = nq * block
    chunk = min(rows, 256)
    for r in range(0, rows, chunk):
        scores = None
        norms = None
        for k in range(nl):
            part = gath[k, r : r + chunk, :]
            prod = nt(part, lib[:, k * cols : (k + 1) * cols])
            wide = part.astype(F32)
            sq = jnp.sum(wide * wide, axis=1, keepdims=True)
            scores = prod if scores is None else scores + prod
            norms = sq if norms is None else norms + sq
        tv_ref[r : r + chunk, :] = (scores * (1.0 / (norms + EPSILON))).astype(BF16)

    tv_copy = pltpu.make_async_copy(tv_ref, tv_hbm, loc_sem.at[7])
    tv_copy.start()
    for g in range(groups):
        first = LANES * g // cap * local_q // 16 * 16
        last = min((LANES * g + LANES - 1) // cap * local_q // 16 * 16 + 16, rows)
        lanes = slice(g * LANES, (g + 1) * LANES)
        chosen = nn(tv_ref[first:last, :], onehot[:, lanes])
        mine = iota((last - first, LANES), 0) + first == pquery[:, lanes]
        prior = jnp.sum(jnp.where(mine, chosen, 0.0), axis=0, keepdims=True)
        score[g] = jnp.where(valid[:, lanes], shape_s[:, lanes] + prior, 0.0)
    score[groups] = jnp.zeros((1, LANES), F32)

    for tq, tl in peers:
        at = lax.div(cap * (tq * nl + tl), LANES)
        remote(score.at[pl.ds(at, 2)], ret_in.at[me_o], send_d, recv_d, tq, tl).start()
    ret_in[me_o] = score[pl.ds(lax.div(cap * me, LANES), 2)]

    take(gath.at[0, pl.ds(0, (nz - 1) * block), :], s1_send)
    take(gath.at[pl.ds(0, nl - 1), pl.ds(0, (nz - 1) * block), :], s2_send)
    take(gath.at[:, pl.ds(0, nz * block), :], sib_send)
    take(atoms_in.at[0, 0, z_rest], send_a)
    take(atoms_in.at[l_rest, 0], send_b)
    take(atoms_in.at[:, 0], send_e)
    take(codes_in.at[d_rest], send_c)
    tv_copy.wait()
    take(ret_in.at[d_rest], recv_d)

    came = jnp.concatenate([ret_in[:, k].reshape(dev, LANES) for k in range(2)], axis=1)
    hi_b, lo_b = split2(came)
    mine = nn(hi_b, rank_b) + nn(lo_b, rank_b)
    final = jnp.sum(jnp.where(owns, mine, 0.0), axis=0, keepdims=True)
    for i in range(local_q):
        line = final[:, i * listed : (i + 1) * listed]
        live = iota((1, listed), 1) < count_ref[i]
        out_ref[i : i + 1, :] = jnp.where(live, line, 0.0)

    take(ret_in.at[d_rest], send_d)


def copy_out(tv_in, score_in, tv_out, score_out, sems):
    copies = [
        pltpu.make_async_copy(tv_in, tv_out, sems.at[0]),
        pltpu.make_async_copy(score_in, score_out, sems.at[1]),
    ]
    for copy in copies:
        copy.start()
    for copy in copies:
        copy.wait()


def hand_over(tv, score):
    return pl.pallas_call(
        copy_out,
        out_shape=(jax.ShapeDtypeStruct(tv.shape, tv.dtype), jax.ShapeDtypeStruct(score.shape, score.dtype)),
        in_specs=[pl.BlockSpec(memory_space=pltpu.VMEM)] * 2,
        out_specs=(pl.BlockSpec(memory_space=pl.ANY), pl.BlockSpec(memory_space=pl.ANY)),
        scratch_shapes=[pltpu.SemaphoreType.DMA((2,))],
    )(tv, score)


def body(nq, nl, query_prints, library_prints, query_atoms, conformer_atoms, candidates, candidate_count, home_row):
    dev = nq * nl
    block, width = query_prints.shape
    own_rows = library_prints.shape[0]
    local_q, listed = candidates.shape
    atoms = query_atoms.shape[1] // 4
    cand_n = local_q * listed
    cap = 2 * ((cand_n + dev - 1) // dev) + 4
    pairs = (dev * cap + LANES - 1) // LANES * LANES
    id_bytes = ((home_row.shape[0] - 1).bit_length() + 7) // 8
    rows = nq * block
    nz = nq // CORES
    limit = 56 * 1024 * 1024
    vm = pltpu.VMEM
    dma = pltpu.SemaphoreType.DMA
    vspec = pl.BlockSpec(memory_space=pltpu.VMEM)
    tv, score = pl.pallas_call(
        functools.partial(kernel, nq, nl, cap, id_bytes),
        out_shape=(
            jax.ShapeDtypeStruct((rows, own_rows), BF16),
            jax.ShapeDtypeStruct((local_q, listed), F32),
        ),
        in_specs=[pl.BlockSpec(memory_space=pltpu.HBM)] * 7,
        out_specs=(pl.BlockSpec(memory_space=pl.ANY), vspec),
        scratch_shapes=[
            vm((rows, own_rows), BF16),
            vm((block, width), BF16),
            vm((local_q, 4 * atoms), F32),
            vm((local_q, listed), I32),
            pltpu.SMEM((local_q,), I32),
            vm((home_row.shape[0] // LANES, LANES), I32),
            vm((own_rows, width), BF16),
            vm((4 * atoms, own_rows), F32),
            vm((nl, rows, width // nl), BF16),
            vm((2 * local_q, LANES), BF16),
            vm((nl, CORES, nz, 2 * local_q, LANES), BF16),
            vm((dev, 2, 1, LANES), I32),
            vm((dev, 2, 1, LANES), I32),
            vm((pairs // LANES + 1, 1, LANES), F32),
            vm((dev, 2, 1, LANES), F32),
            vm((4 * atoms, own_rows), F32),
            vm((4 * atoms, rows), F32),
            vm((4 * atoms, LANES), F32),
            vm((4 * atoms + 8, pairs), F32),
            vm((4 * atoms + 8, pairs), F32),
            vm((own_rows, pairs), BF16),
            vm((rows, pairs), BF16),
            vm((1, own_rows), F32),
            vm((1, pairs), F32),
            dma((8,)),
            dma, dma((nz,)),
            dma, dma,
            dma, dma((nz, nl)),
            dma, dma, dma, dma, dma, dma, dma, dma, dma, dma,
            pltpu.SemaphoreType.REGULAR,
        ],
        compiler_params=pltpu.CompilerParams(
            collective_id=0, has_side_effects=True, vmem_limit_bytes=limit
        ),
    )(
        query_prints, library_prints, query_atoms, conformer_atoms.T, candidates, candidate_count,
        home_row.reshape(-1, LANES),
    )
    return hand_over(tv, score)


def solution(mesh):
    return jax.shard_map(
        functools.partial(body, mesh.shape["qry"], mesh.shape["lib"]),
        mesh=mesh,
        in_specs=(
            P("qry", None),
            P(("lib", "qry"), None),
            P(("qry", "lib"), None),
            P(("lib", "qry"), None),
            P(("qry", "lib"), None),
            P(("qry", "lib")),
            P(),
        ),
        out_specs=(P(None, ("lib", "qry")), P(("qry", "lib"), None)),
        check_vma=False,
    )
```

```python
import functools
import math

import jax
import jax.numpy as jnp
from jax import lax
from jax.experimental import pallas as pl
from jax.experimental.pallas import tpu as pltpu
from jax.sharding import PartitionSpec as P

SHARPNESS = 0.8
EPSILON = 1e-06
LANES = 128
CORES = 2
SCALE = SHARPNESS * math.log2(math.e)
ROOT = math.sqrt(2.0 * SCALE)

F32 = jnp.float32
BF16 = jnp.bfloat16
I32 = jnp.int32


def nt(a, b):
    return lax.dot_general(a, b, (((1,), (1,)), ((), ())), preferred_element_type=F32)


def nn(a, b):
    return lax.dot_general(a, b, (((1,), (0,)), ((), ())), preferred_element_type=F32)


def split2(x):
    hi = x.astype(BF16)
    return hi, (x - hi.astype(F32)).astype(BF16)


def iota(shape, dim):
    return lax.broadcasted_iota(I32, shape, dim)


def fdiv(x, by):
    return jnp.floor((x.astype(F32) + 0.5) * (1.0 / by)).astype(I32)


def prepare(x, y, z, w):
    norm = SCALE * (x * x + y * y + z * z)
    return x * ROOT, y * ROOT, z * ROOT, w * jnp.exp2(-norm)


def self_overlap(ref, lanes, atoms):
    blocks = atoms // 8
    comp = [[ref[pl.ds(c * atoms + 8 * i, 8), lanes] for i in range(blocks)] for c in range(4)]
    total = None
    diag = [None] * blocks
    off = [None] * blocks
    for a in range(atoms):
        xa, ya, za, wa = (ref[pl.ds(c * atoms + a, 1), lanes] for c in range(4))
        wa2 = wa + wa
        for i in range(a // 8, blocks):
            e = jnp.exp2(xa * comp[0][i] + ya * comp[1][i] + za * comp[2][i])
            if i == a // 8:
                diag[i] = wa * e if diag[i] is None else diag[i] + wa * e
            else:
                off[i] = wa2 * e if off[i] is None else off[i] + wa2 * e
    for i in range(blocks):
        part = diag[i] if off[i] is None else diag[i] + off[i]
        part = part * comp[3][i]
        total = part if total is None else total + part
    return jnp.sum(total, axis=0, keepdims=True)


def cross_overlap(qref, cref, lanes, atoms):
    comp = [cref[pl.ds(c * atoms, atoms), lanes] for c in range(4)]
    acc = None
    for a in range(atoms):
        xa, ya, za, wa = (qref[pl.ds(c * atoms + a, 1), lanes] for c in range(4))
        e = wa * jnp.exp2(xa * comp[0] + ya * comp[1] + za * comp[2])
        acc = e if acc is None else acc + e
    return jnp.sum(acc * comp[3], axis=0, keepdims=True)


def flip(x, bits):
    step, out = 1, x
    while step < 256:
        one = lax.rem(lax.div(x, step), 2)
        other = lax.rem(lax.div(bits, step), 2) if not isinstance(bits, int) else (bits // step) % 2
        out = out + other * (1 - 2 * one) * step
        step *= 2
        if isinstance(bits, int) and step > bits:
            break
    return out


def kernel(
    nq, nl, cap, id_bytes,
    qp_hbm, lib_hbm, qa_hbm, conf_hbm, cand_hbm, home_hbm,
    tv_hbm, ret_in, meta_hbm,
    tv_ref,
    qp_ref, qa_ref, cand_ref, home_ref,
    lib, turned, conf, gath, pack, atoms_in, codes_out, codes_in, score, meta,
    confp, qprep, ownprep, pairs_c, pairs_q, inv_ref, onehot, qonehot, cself, shape_s,
    loc_sem, s1_send, s1_recv, sib_send, sib_recv, s2_send, s2_recv,
    send_a, recv_a, send_b, recv_b, send_c, recv_c, send_d, recv_d, send_e, recv_e, ready,
):
    q = lax.axis_index("qry")
    l = lax.axis_index("lib")
    dev = nq * nl
    me = q * nl + l
    me_o = l * nq + q
    nz = nq // CORES
    z, c = lax.div(q, CORES), lax.rem(q, CORES)
    sib = z * CORES + (1 - c)
    own_rows = lib.shape[0]
    block = qp_ref.shape[0]
    cols = gath.shape[2]
    local_q, listed = cand_ref.shape
    cand_n = local_q * listed
    atoms = qa_ref.shape[1] // 4
    half = 2 * atoms
    pairs = onehot.shape[1]
    groups = pairs // LANES

    spread = [(d, e) for d in range(nq) for e in range(nl) if d or e]
    spread.sort(key=lambda o: -(o[0] // CORES + bin(o[1]).count("1")))
    near = [(q, flip(l, e)) for e in range(nl - 1, 0, -1)] + [(flip(q, d), l) for d in range(nq - 1, 0, -1)]
    peers = [(flip(q, d) if d else q, flip(l, e) if e else l) for d, e in spread]

    def take(ref, sem):
        pltpu.make_async_copy(ref, ref, sem).wait()

    def remote(src, dst, ssem, rsem, dq, dl):
        return pltpu.make_async_remote_copy(
            src_ref=src, dst_ref=dst, send_sem=ssem, recv_sem=rsem,
            device_id={"qry": dq, "lib": dl}, device_id_type=pl.DeviceIdType.MESH,
        )

    barrier = pltpu.get_barrier_semaphore()
    loads = [
        pltpu.make_async_copy(src, dst, loc_sem.at[2 + n])
        for n, (src, dst) in enumerate(
            ((qa_hbm, qa_ref), (cand_hbm, cand_ref), (home_hbm, home_ref), (qp_hbm, qp_ref))
        )
    ]
    for load in loads:
        load.start()
    lib_copy = pltpu.make_async_copy(lib_hbm, lib, loc_sem.at[0])
    conf_copy = pltpu.make_async_copy(conf_hbm, conf, loc_sem.at[1])
    conf_copy.start()
    lib_copy.start()

    for tq, tl in near:
        pl.semaphore_signal(
            barrier, inc=1, device_id={"qry": tq, "lib": tl}, device_id_type=pl.DeviceIdType.MESH
        )

    loads[3].wait()
    loads[0].wait()

    qa = qa_ref[...]
    zero = jnp.zeros((local_q, LANES - half), F32)
    top = jnp.concatenate([qa[:, :half], zero], axis=1)
    low = jnp.concatenate([qa[:, half:], zero], axis=1)
    fill = jnp.zeros((LANES - local_q, LANES), F32)
    top_t = jnp.transpose(jnp.concatenate([top, fill], axis=0))
    low_t = jnp.transpose(jnp.concatenate([low, fill], axis=0))
    comps = prepare(top_t[:atoms], top_t[atoms:half], low_t[:atoms], low_t[atoms:half])
    for i in range(4):
        ownprep[i * atoms : (i + 1) * atoms] = comps[i]
    own_self = self_overlap(ownprep, pl.ds(0, LANES), atoms)
    lane_at = iota((local_q, LANES), 1)
    own_col = jnp.sum(
        jnp.where(lane_at == iota((local_q, LANES), 0), own_self, 0.0), axis=1, keepdims=True
    )
    own_hi = own_col.astype(BF16).astype(F32)
    prints = qp_ref[...].astype(F32)
    squares = jnp.sum(prints * prints, axis=1, keepdims=True)
    norm = jnp.zeros((local_q, 1), F32)
    for k in range(nl):
        norm = norm + jnp.where(l == k, squares[k * local_q : (k + 1) * local_q], 0.0)
    norm_hi = norm.astype(BF16).astype(F32)
    norm_mid = (norm - norm_hi).astype(BF16).astype(F32)
    extra = (own_hi, own_col - own_hi, norm_hi, norm_mid, norm - norm_hi - norm_mid)
    for k, column in enumerate(extra):
        low = jnp.where(lane_at == half + k, column, low)
    pack[...] = jnp.concatenate([top, low], axis=0).astype(BF16)

    pl.semaphore_wait(barrier, nq + nl - 2)
    for e in range(nl - 1, 0, -1):
        pl.semaphore_signal(
            ready, inc=1, device_id={"qry": q, "lib": flip(l, e)}, device_id_type=pl.DeviceIdType.MESH
        )

    def piece(bq, k):
        return gath.at[k, pl.ds(pl.multiple_of(bq * block, block), block), :]

    def from_z(d):
        return flip(z, d) * CORES + c

    def stage1(d):
        return remote(
            qp_ref.at[:, pl.ds(pl.multiple_of(l * cols, cols), cols)], piece(q, l),
            s1_send, s1_recv.at[d], from_z(d), l,
        )

    def stage2(d, e):
        there = piece(from_z(d), l)
        return remote(there, there, s2_send, s2_recv.at[d, e], q, flip(l, e))

    def to_sib(bq, k):
        there = piece(bq, k)
        return remote(there, there, sib_send, sib_recv, sib, l)

    def atoms_to(k, dq, dl, ssem, rsem):
        there = atoms_in.at[k, c]
        return remote(there, there, ssem, rsem, dq, dl)

    for d in range(nz - 1, 0, -1):
        remote(pack, atoms_in.at[l, c, z], send_a, recv_a, from_z(d), l).start()
    for d in range(1, nz):
        stage1(d).start()
    for k in range(nl):
        gath[k, pl.ds(pl.multiple_of(q * block, block), block), :] = qp_ref[:, k * cols : (k + 1) * cols]
    for k in range(nl):
        to_sib(q, k).start()
    atoms_in[l, c, z] = pack[...]

    for load in loads[1:3]:
        load.wait()

    ids = jnp.concatenate([cand_ref[pl.ds(i, 1), :] for i in range(local_q)], axis=1)
    table = home_ref[...]
    trows = table.shape[0]
    pieces = [
        jnp.transpose(((table >> (8 * k)) & 255).astype(F32)).astype(BF16) for k in range(id_bytes)
    ]
    row_hot = jnp.where(iota((trows, cand_n), 0) == (ids >> 7), 1.0, 0.0).astype(BF16)
    lane_hot = iota((LANES, cand_n), 0) == (ids & 127)
    stored = jnp.zeros((1, cand_n), I32)
    for k in range(id_bytes):
        found = nn(pieces[k], row_hot)
        byte = jnp.sum(jnp.where(lane_hot, found, 0.0), axis=0, keepdims=True)
        stored = stored + (byte.astype(I32) << (8 * k))
    owner = fdiv(stored, own_rows)
    slot = stored - owner * own_rows

    owns = iota((dev, cand_n), 0) == owner
    owns_b = jnp.where(owns, 1.0, 0.0).astype(BF16)
    tri = jnp.where(iota((cand_n, cand_n), 0) < iota((cand_n, cand_n), 1), 1.0, 0.0).astype(BF16)
    before = nn(owns_b, tri)
    rank = jnp.sum(jnp.where(owns, before, 0.0), axis=0, keepdims=True).astype(I32)
    my_off = lax.rem(cap * me, LANES)
    meta[0] = owner
    meta[1] = rank + my_off
    meta_copy = pltpu.make_async_copy(meta, meta_hbm, loc_sem.at[6])
    meta_copy.start()
    rank_b = jnp.where(iota((2 * LANES, cand_n), 0) == rank + my_off, 1.0, 0.0).astype(BF16)
    code = slot * local_q + fdiv(iota((1, cand_n), 1), listed) + 1
    lo = (code & 127).astype(F32)
    hi = (code >> 7).astype(F32)
    left = jnp.concatenate([jnp.where(owns, lo, 0.0), jnp.where(owns, hi, 0.0)], axis=0).astype(BF16)
    sums = nt(left, rank_b).astype(I32)
    codes = sums[:dev] + (sums[dev:] << 7)
    for o in range(dev):
        for k in range(2):
            codes_out[o, k] = codes[o : o + 1, k * LANES : (k + 1) * LANES]

    pl.semaphore_wait(ready, nl - 1)
    for tq, tl in peers:
        remote(codes_out.at[tl * nq + tq], codes_in.at[me], send_c, recv_c, tq, tl).start()
    codes_in[me] = codes_out[me_o]

    conf_copy.wait()
    comps = prepare(*(conf[i * atoms : (i + 1) * atoms] for i in range(4)))
    for i in range(4):
        confp[i * atoms : (i + 1) * atoms] = comps[i]

    def self_step(g, carry):
        lanes = pl.ds(pl.multiple_of(g * LANES, LANES), LANES)
        cself[0:1, lanes] = self_overlap(confp, lanes, atoms)
        return carry

    selves = own_rows // LANES
    lax.fori_loop(0, selves, self_step, 0)

    z_rest = pl.ds(0, nz - 1)
    l_rest = pl.ds(0, nl - 1)
    d_rest = pl.ds(0, dev - 1)

    lib_copy.wait()
    blocks = own_rows // LANES
    turns = [n * blocks // nz for n in range(nz + 1)]

    def turn(n):
        for b in range(turns[n], turns[n + 1]):
            at = slice(b * LANES, (b + 1) * LANES)
            turned[:, at] = jnp.transpose(lib[at, :])

    turn(0)
    take(atoms_in.at[0, 0, z_rest], recv_a)
    for e in range(nl - 1, 0, -1):
        atoms_to(l, q, flip(l, e), send_b, recv_b).start()
    atoms_to(l, sib, l, send_e, recv_e).start()
    for d in range(1, nz):
        stage1(d).wait_recv()
        for e in range(nl - 1, 0, -1):
            stage2(d, e).start()
        to_sib(from_z(d), l).start()
        turn(d)

    take(codes_in.at[d_rest], recv_c)
    parts = [None] * groups
    for s in range(dev):
        g = cap * s // LANES
        for k in range(2):
            if g + k < groups:
                row = codes_in[s, k]
                parts[g + k] = row if parts[g + k] is None else parts[g + k] + row
    none = jnp.zeros((1, LANES), I32)
    pcode = jnp.concatenate([none if p is None else p for p in parts], axis=1)
    valid = pcode > 0
    pcode = jnp.maximum(pcode - 1, 0)
    pslot = fdiv(pcode, local_q)
    source = fdiv(iota((1, pairs), 1), cap)
    which = pcode - pslot * local_q
    pquery = source * local_q + which
    src_q, src_l = source // nl, source % nl
    held = ((src_l * CORES + src_q % CORES) * nz + src_q // CORES) * local_q + which
    onehot[...] = jnp.where(iota((own_rows, pairs), 0) == pslot, 1.0, 0.0).astype(BF16)
    qonehot[...] = jnp.where(iota((dev * local_q, pairs), 0) == held, 1.0, 0.0).astype(BF16)

    take(atoms_in.at[l_rest, 0], recv_b)
    for e in range(nl - 1, 0, -1):
        atoms_to(flip(l, e), sib, l, send_e, recv_e).start()

    self_hi, self_lo = split2(cself[...])
    pad = jnp.zeros((14, own_rows), BF16)
    found = nn(jnp.concatenate([conf[...].astype(BF16), self_hi, self_lo, pad], axis=0), onehot[...])
    comps = prepare(*(found[i * atoms : (i + 1) * atoms] for i in range(4)))
    for i in range(4):
        pairs_c[i * atoms : (i + 1) * atoms] = comps[i]
    pairs_c[4 * atoms : 4 * atoms + 1] = found[4 * atoms : 4 * atoms + 1] + found[4 * atoms + 1 : 4 * atoms + 2]

    take(atoms_in.at[:, 0], recv_e)
    raw = atoms_in[...].reshape(dev, 2 * local_q, LANES).astype(F32)
    q_top = jnp.transpose(raw[:, :local_q].reshape(dev * local_q, LANES))
    q_low = jnp.transpose(raw[:, local_q:].reshape(dev * local_q, LANES))
    comps = prepare(q_top[:atoms], q_top[atoms:half], q_low[:atoms], q_low[atoms:half])
    for i in range(4):
        qprep[i * atoms : (i + 1) * atoms] = comps[i]
    qself = q_low[half : half + 1] + q_low[half + 1 : half + 2]
    pad = jnp.zeros((7, dev * local_q), F32)
    hi_q, lo_q = split2(jnp.concatenate([qprep[...], qself, pad], axis=0))
    pairs_q[...] = nn(hi_q, qonehot[...]) + nn(lo_q, qonehot[...])
    inverse = raw[:, local_q:, half + 2 : half + 3] + raw[:, local_q:, half + 3 : half + 4]
    inverse = 1.0 / (inverse + raw[:, local_q:, half + 4 : half + 5] + EPSILON)
    for s in range(dev):
        there = (s % nl * CORES + s // nl % CORES) * nz + s // nl // CORES
        inv_ref[s * local_q : (s + 1) * local_q, :] = inverse[there]

    n_far = (nz - 1) * (nl - 1)
    each = (2 * n_far + groups - 1) // groups

    def onward(n):
        d = 1 + lax.div(n, nl - 1)
        e = nl - 1 - lax.rem(n, nl - 1)
        stage2(d, e).wait_recv()
        to_sib(from_z(d), flip(l, e)).start()

    def cross_step(g, carry):
        for k in range(each):
            n = g * each + k
            if groups * each == n_far:
                onward(n)
            else:
                pl.when(n < n_far)(functools.partial(onward, n))
        lanes = pl.ds(pl.multiple_of(g * LANES, LANES), LANES)
        cross = cross_overlap(pairs_q, pairs_c, lanes, atoms)
        selves = pairs_q[4 * atoms : 4 * atoms + 1, lanes] + pairs_c[4 * atoms : 4 * atoms + 1, lanes]
        shape_s[0:1, lanes] = cross / (selves - cross)
        return carry

    lax.fori_loop(0, groups, cross_step, 0)

    take(gath.at[:, pl.ds(0, nz * block), :], sib_recv)

    rows = nq * block
    chunk = min(rows, 256)
    for r in range(0, rows, chunk):
        scores = None
        for k in range(nl):
            part = gath[k, r : r + chunk, :]
            prod = nn(part, turned[k * cols : (k + 1) * cols, :])
            scores = prod if scores is None else scores + prod
        tv_ref[r : r + chunk, :] = (scores * inv_ref[r : r + chunk, :]).astype(BF16)

    tv_copy = pltpu.make_async_copy(tv_ref, tv_hbm, loc_sem.at[7])
    tv_copy.start()
    for g in range(groups):
        first = LANES * g // cap * local_q // 16 * 16
        last = min((LANES * g + LANES - 1) // cap * local_q // 16 * 16 + 16, rows)
        lanes = slice(g * LANES, (g + 1) * LANES)
        chosen = nn(tv_ref[first:last, :], onehot[:, lanes])
        mine = iota((last - first, LANES), 0) + first == pquery[:, lanes]
        prior = jnp.sum(jnp.where(mine, chosen, 0.0), axis=0, keepdims=True)
        score[g] = jnp.where(valid[:, lanes], shape_s[:, lanes] + prior, 0.0)
    score[groups] = jnp.zeros((1, LANES), F32)

    for tq, tl in peers:
        at = lax.div(cap * (tq * nl + tl), LANES)
        remote(score.at[pl.ds(at, 2)], ret_in.at[me_o], send_d, recv_d, tq, tl).start()
    own_copy = pltpu.make_async_copy(score.at[pl.ds(lax.div(cap * me, LANES), 2)], ret_in.at[me_o], loc_sem.at[5])
    own_copy.start()

    take(gath.at[0, pl.ds(0, (nz - 1) * block), :], s1_send)
    take(gath.at[pl.ds(0, nl - 1), pl.ds(0, (nz - 1) * block), :], s2_send)
    take(gath.at[:, pl.ds(0, nz * block), :], sib_send)
    take(atoms_in.at[0, 0, z_rest], send_a)
    take(atoms_in.at[l_rest, 0], send_b)
    take(atoms_in.at[:, 0], send_e)
    take(codes_in.at[d_rest], send_c)
    tv_copy.wait()
    meta_copy.wait()
    own_copy.wait()
    take(ret_in.at[d_rest], recv_d)
    take(ret_in.at[d_rest], send_d)


def finish(tv_in, ret_in, meta, count, tv_out, out_ref, sem):
    copy = pltpu.make_async_copy(tv_in, tv_out, sem)
    copy.start()
    dev = ret_in.shape[0]
    local_q, listed = out_ref.shape
    cand_n = local_q * listed
    owns = iota((dev, cand_n), 0) == meta[0]
    rank_b = jnp.where(iota((2 * LANES, cand_n), 0) == meta[1], 1.0, 0.0).astype(BF16)
    came = jnp.concatenate([ret_in[:, k].reshape(dev, LANES) for k in range(2)], axis=1)
    hi_b, lo_b = split2(came)
    mine = nn(hi_b, rank_b) + nn(lo_b, rank_b)
    final = jnp.sum(jnp.where(owns, mine, 0.0), axis=0, keepdims=True)
    for i in range(local_q):
        line = final[:, i * listed : (i + 1) * listed]
        live = iota((1, listed), 1) < count[i]
        out_ref[i : i + 1, :] = jnp.where(live, line, 0.0)
    copy.wait()


def hand_over(tv, ret, meta, count, out_shape):
    vspec = pl.BlockSpec(memory_space=pltpu.VMEM)
    return pl.pallas_call(
        finish,
        out_shape=(jax.ShapeDtypeStruct(tv.shape, tv.dtype), jax.ShapeDtypeStruct(out_shape, F32)),
        in_specs=[vspec, vspec, vspec, pl.BlockSpec(memory_space=pltpu.SMEM)],
        out_specs=(pl.BlockSpec(memory_space=pl.ANY), vspec),
        scratch_shapes=[pltpu.SemaphoreType.DMA],
    )(tv, ret, meta, count)


def body(nq, nl, query_prints, library_prints, query_atoms, conformer_atoms, candidates, candidate_count, home_row):
    dev = nq * nl
    block, width = query_prints.shape
    own_rows = library_prints.shape[0]
    local_q, listed = candidates.shape
    atoms = query_atoms.shape[1] // 4
    cand_n = local_q * listed
    cap = 2 * ((cand_n + dev - 1) // dev) + 4
    pairs = (dev * cap + LANES - 1) // LANES * LANES
    id_bytes = ((home_row.shape[0] - 1).bit_length() + 7) // 8
    rows = nq * block
    nz = nq // CORES
    limit = 56 * 1024 * 1024
    vm = pltpu.VMEM
    dma = pltpu.SemaphoreType.DMA
    hspec = pl.BlockSpec(memory_space=pl.ANY)
    tv, ret, meta = pl.pallas_call(
        functools.partial(kernel, nq, nl, cap, id_bytes),
        out_shape=(
            jax.ShapeDtypeStruct((rows, own_rows), BF16),
            jax.ShapeDtypeStruct((dev, 2, 1, LANES), F32),
            jax.ShapeDtypeStruct((2, 1, cand_n), I32),
        ),
        in_specs=[pl.BlockSpec(memory_space=pltpu.HBM)] * 6,
        out_specs=(hspec, hspec, hspec),
        scratch_shapes=[
            vm((rows, own_rows), BF16),
            vm((block, width), BF16),
            vm((local_q, 4 * atoms), F32),
            vm((local_q, listed), I32),
            vm((home_row.shape[0] // LANES, LANES), I32),
            vm((own_rows, width), BF16),
            vm((width, own_rows), BF16),
            vm((4 * atoms, own_rows), F32),
            vm((nl, rows, width // nl), BF16),
            vm((2 * local_q, LANES), BF16),
            vm((nl, CORES, nz, 2 * local_q, LANES), BF16),
            vm((dev, 2, 1, LANES), I32),
            vm((dev, 2, 1, LANES), I32),
            vm((pairs // LANES + 1, 1, LANES), F32),
            vm((2, 1, cand_n), I32),
            vm((4 * atoms, own_rows), F32),
            vm((4 * atoms, rows), F32),
            vm((4 * atoms, LANES), F32),
            vm((4 * atoms + 8, pairs), F32),
            vm((4 * atoms + 8, pairs), F32),
            vm((rows, 1), F32),
            vm((own_rows, pairs), BF16),
            vm((rows, pairs), BF16),
            vm((1, own_rows), F32),
            vm((1, pairs), F32),
            dma((8,)),
            dma, dma((nz,)),
            dma, dma,
            dma, dma((nz, nl)),
            dma, dma, dma, dma, dma, dma, dma, dma, dma, dma,
            pltpu.SemaphoreType.REGULAR,
        ],
        compiler_params=pltpu.CompilerParams(
            collective_id=0, has_side_effects=True, vmem_limit_bytes=limit
        ),
    )(
        query_prints, library_prints, query_atoms, conformer_atoms.T, candidates,
        home_row.reshape(-1, LANES),
    )
    return hand_over(tv, ret, meta, candidate_count, (local_q, listed))


def solution(mesh):
    return jax.shard_map(
        functools.partial(body, mesh.shape["qry"], mesh.shape["lib"]),
        mesh=mesh,
        in_specs=(
            P("qry", None),
            P(("lib", "qry"), None),
            P(("qry", "lib"), None),
            P(("lib", "qry"), None),
            P(("qry", "lib"), None),
            P(("qry", "lib")),
            P(),
        ),
        out_specs=(P(None, ("lib", "qry")), P(("qry", "lib"), None)),
        check_vma=False,
    )
```

```python
import functools
import math

import jax
import jax.numpy as jnp
from jax import lax
from jax.experimental import pallas as pl
from jax.experimental.pallas import tpu as pltpu
from jax.sharding import PartitionSpec as P

SHARPNESS = 0.8
EPSILON = 1e-06
LANES = 128
CORES = 2
SCALE = SHARPNESS * math.log2(math.e)
ROOT = math.sqrt(2.0 * SCALE)

F32 = jnp.float32
BF16 = jnp.bfloat16
I32 = jnp.int32


def nt(a, b):
    return lax.dot_general(a, b, (((1,), (1,)), ((), ())), preferred_element_type=F32)


def nn(a, b):
    return lax.dot_general(a, b, (((1,), (0,)), ((), ())), preferred_element_type=F32)


def split2(x):
    hi = x.astype(BF16)
    return hi, (x - hi.astype(F32)).astype(BF16)


def iota(shape, dim):
    return lax.broadcasted_iota(I32, shape, dim)


def fdiv(x, by):
    return jnp.floor((x.astype(F32) + 0.5) * (1.0 / by)).astype(I32)


def prepare(x, y, z, w):
    norm = SCALE * (x * x + y * y + z * z)
    return x * ROOT, y * ROOT, z * ROOT, w * jnp.exp2(-norm)


def self_overlap(ref, lanes, atoms):
    blocks = atoms // 8
    comp = [[ref[pl.ds(c * atoms + 8 * i, 8), lanes] for i in range(blocks)] for c in range(4)]
    total = None
    diag = [None] * blocks
    off = [None] * blocks
    for a in range(atoms):
        xa, ya, za, wa = (ref[pl.ds(c * atoms + a, 1), lanes] for c in range(4))
        wa2 = wa + wa
        for i in range(a // 8, blocks):
            e = jnp.exp2(xa * comp[0][i] + ya * comp[1][i] + za * comp[2][i])
            if i == a // 8:
                diag[i] = wa * e if diag[i] is None else diag[i] + wa * e
            else:
                off[i] = wa2 * e if off[i] is None else off[i] + wa2 * e
    for i in range(blocks):
        part = diag[i] if off[i] is None else diag[i] + off[i]
        part = part * comp[3][i]
        total = part if total is None else total + part
    return jnp.sum(total, axis=0, keepdims=True)


def cross_overlap(qref, cref, lanes, atoms):
    comp = [cref[pl.ds(c * atoms, atoms), lanes] for c in range(4)]
    acc = None
    for a in range(atoms):
        xa, ya, za, wa = (qref[pl.ds(c * atoms + a, 1), lanes] for c in range(4))
        e = wa * jnp.exp2(xa * comp[0] + ya * comp[1] + za * comp[2])
        acc = e if acc is None else acc + e
    return jnp.sum(acc * comp[3], axis=0, keepdims=True)


def flip(x, bits):
    step, out = 1, x
    while step < 256:
        one = lax.rem(lax.div(x, step), 2)
        other = lax.rem(lax.div(bits, step), 2) if not isinstance(bits, int) else (bits // step) % 2
        out = out + other * (1 - 2 * one) * step
        step *= 2
        if isinstance(bits, int) and step > bits:
            break
    return out


def kernel(
    nq, nl, cap, id_bytes,
    qp_hbm, lib_hbm, qa_hbm, conf_hbm, cand_hbm, home_hbm,
    tv_hbm, ret_in, meta_hbm,
    tv_ref,
    qp_ref, qa_ref, cand_ref, home_ref,
    lib, turned, conf, gath, pack, atoms_in, codes_out, codes_in, score, meta,
    confp, ownprep, pairs_c, pairs_q, inv_ref, onehot, qonehot, cself, shape_s,
    loc_sem, s1_send, s1_recv, sib_send, sib_recv, s2_send, s2_recv,
    send_a, recv_a, send_b, recv_b, send_c, recv_c, send_d, recv_d, send_e, recv_e, ready,
):
    q = lax.axis_index("qry")
    l = lax.axis_index("lib")
    dev = nq * nl
    me = q * nl + l
    me_o = l * nq + q
    nz = nq // CORES
    z, c = lax.div(q, CORES), lax.rem(q, CORES)
    sib = z * CORES + (1 - c)
    own_rows = lib.shape[0]
    block = qp_ref.shape[0]
    cols = gath.shape[2]
    local_q, listed = cand_ref.shape
    cand_n = local_q * listed
    atoms = qa_ref.shape[1] // 4
    half = 2 * atoms
    pairs = onehot.shape[1]
    groups = pairs // LANES

    spread = [(d, e) for d in range(nq) for e in range(nl) if d or e]
    spread.sort(key=lambda o: -(o[0] // CORES + bin(o[1]).count("1")))
    near = [(q, flip(l, e)) for e in range(nl - 1, 0, -1)] + [(flip(q, d), l) for d in range(nq - 1, 0, -1)]
    peers = [(flip(q, d) if d else q, flip(l, e) if e else l) for d, e in spread]

    def take(ref, sem):
        pltpu.make_async_copy(ref, ref, sem).wait()

    def remote(src, dst, ssem, rsem, dq, dl):
        return pltpu.make_async_remote_copy(
            src_ref=src, dst_ref=dst, send_sem=ssem, recv_sem=rsem,
            device_id={"qry": dq, "lib": dl}, device_id_type=pl.DeviceIdType.MESH,
        )

    barrier = pltpu.get_barrier_semaphore()
    loads = [
        pltpu.make_async_copy(src, dst, loc_sem.at[2 + n])
        for n, (src, dst) in enumerate(
            ((qa_hbm, qa_ref), (cand_hbm, cand_ref), (home_hbm, home_ref), (qp_hbm, qp_ref))
        )
    ]
    for load in loads:
        load.start()
    lib_copy = pltpu.make_async_copy(lib_hbm, lib, loc_sem.at[0])
    conf_copy = pltpu.make_async_copy(conf_hbm, conf, loc_sem.at[1])
    conf_copy.start()
    lib_copy.start()

    for tq, tl in near:
        pl.semaphore_signal(
            barrier, inc=1, device_id={"qry": tq, "lib": tl}, device_id_type=pl.DeviceIdType.MESH
        )

    loads[3].wait()
    loads[0].wait()

    qa = qa_ref[...]
    zero = jnp.zeros((local_q, LANES - half), F32)
    top = jnp.concatenate([qa[:, :half], zero], axis=1)
    low = jnp.concatenate([qa[:, half:], zero], axis=1)
    fill = jnp.zeros((LANES - local_q, LANES), F32)
    top_t = jnp.transpose(jnp.concatenate([top, fill], axis=0))
    low_t = jnp.transpose(jnp.concatenate([low, fill], axis=0))
    comps = prepare(top_t[:atoms], top_t[atoms:half], low_t[:atoms], low_t[atoms:half])
    for i in range(4):
        ownprep[i * atoms : (i + 1) * atoms] = comps[i]
    own_self = self_overlap(ownprep, pl.ds(0, LANES), atoms)
    lane_at = iota((local_q, LANES), 1)
    own_col = jnp.sum(
        jnp.where(lane_at == iota((local_q, LANES), 0), own_self, 0.0), axis=1, keepdims=True
    )
    own_hi = own_col.astype(BF16).astype(F32)
    prints = qp_ref[...].astype(F32)
    squares = jnp.sum(prints * prints, axis=1, keepdims=True)
    norm = jnp.zeros((local_q, 1), F32)
    for k in range(nl):
        norm = norm + jnp.where(l == k, squares[k * local_q : (k + 1) * local_q], 0.0)
    norm_hi = norm.astype(BF16).astype(F32)
    norm_mid = (norm - norm_hi).astype(BF16).astype(F32)
    extra = (own_hi, own_col - own_hi, norm_hi, norm_mid, norm - norm_hi - norm_mid)
    for k, column in enumerate(extra):
        low = jnp.where(lane_at == half + k, column, low)
    pack[...] = jnp.concatenate([top, low], axis=0).astype(BF16)

    pl.semaphore_wait(barrier, nq + nl - 2)
    for e in range(nl - 1, 0, -1):
        pl.semaphore_signal(
            ready, inc=1, device_id={"qry": q, "lib": flip(l, e)}, device_id_type=pl.DeviceIdType.MESH
        )

    def piece(bq, k):
        return gath.at[k, pl.ds(pl.multiple_of(bq * block, block), block), :]

    def from_z(d):
        return flip(z, d) * CORES + c

    def stage1(d):
        return remote(
            qp_ref.at[:, pl.ds(pl.multiple_of(l * cols, cols), cols)], piece(q, l),
            s1_send, s1_recv.at[d], from_z(d), l,
        )

    def stage2(d, e):
        there = piece(from_z(d), l)
        return remote(there, there, s2_send, s2_recv.at[d, e], q, flip(l, e))

    def to_sib(bq, k, late):
        there = piece(bq, k)
        return remote(there, there, sib_send, sib_recv.at[late], sib, l)

    def atoms_to(k, dq, dl, ssem, rsem):
        there = atoms_in.at[k, c]
        return remote(there, there, ssem, rsem, dq, dl)

    for d in range(nz - 1, 0, -1):
        remote(pack, atoms_in.at[l, c, z], send_a, recv_a, from_z(d), l).start()
    for d in range(1, nz):
        stage1(d).start()
    for k in range(nl):
        gath[k, pl.ds(pl.multiple_of(q * block, block), block), :] = qp_ref[:, k * cols : (k + 1) * cols]
    atoms_in[l, c, z] = pack[...]

    for load in loads[1:3]:
        load.wait()

    ids = jnp.concatenate([cand_ref[pl.ds(i, 1), :] for i in range(local_q)], axis=1)
    table = home_ref[...]
    trows = table.shape[0]
    pieces = [
        jnp.transpose(((table >> (8 * k)) & 255).astype(F32)).astype(BF16) for k in range(id_bytes)
    ]
    row_hot = jnp.where(iota((trows, cand_n), 0) == (ids >> 7), 1.0, 0.0).astype(BF16)
    lane_hot = iota((LANES, cand_n), 0) == (ids & 127)
    stored = jnp.zeros((1, cand_n), I32)
    for k in range(id_bytes):
        found = nn(pieces[k], row_hot)
        byte = jnp.sum(jnp.where(lane_hot, found, 0.0), axis=0, keepdims=True)
        stored = stored + (byte.astype(I32) << (8 * k))
    owner = fdiv(stored, own_rows)
    slot = stored - owner * own_rows

    owns = iota((dev, cand_n), 0) == owner
    owns_b = jnp.where(owns, 1.0, 0.0).astype(BF16)
    tri = jnp.where(iota((cand_n, cand_n), 0) < iota((cand_n, cand_n), 1), 1.0, 0.0).astype(BF16)
    before = nn(owns_b, tri)
    rank = jnp.sum(jnp.where(owns, before, 0.0), axis=0, keepdims=True).astype(I32)
    my_off = lax.rem(cap * me, LANES)
    meta[0] = owner
    meta[1] = rank + my_off
    meta_copy = pltpu.make_async_copy(meta, meta_hbm, loc_sem.at[6])
    meta_copy.start()
    rank_b = jnp.where(iota((2 * LANES, cand_n), 0) == rank + my_off, 1.0, 0.0).astype(BF16)
    code = slot * local_q + fdiv(iota((1, cand_n), 1), listed) + 1
    lo = (code & 127).astype(F32)
    hi = (code >> 7).astype(F32)
    left = jnp.concatenate([jnp.where(owns, lo, 0.0), jnp.where(owns, hi, 0.0)], axis=0).astype(BF16)
    sums = nt(left, rank_b).astype(I32)
    codes = sums[:dev] + (sums[dev:] << 7)
    for o in range(dev):
        for k in range(2):
            codes_out[o, k] = codes[o : o + 1, k * LANES : (k + 1) * LANES]

    pl.semaphore_wait(ready, nl - 1)
    for tq, tl in peers:
        remote(codes_out.at[tl * nq + tq], codes_in.at[me], send_c, recv_c, tq, tl).start()
    for k in range(nl):
        to_sib(q, k, 0).start()
    codes_in[me] = codes_out[me_o]

    conf_copy.wait()
    comps = prepare(*(conf[i * atoms : (i + 1) * atoms] for i in range(4)))
    for i in range(4):
        confp[i * atoms : (i + 1) * atoms] = comps[i]

    def self_step(g, carry):
        lanes = pl.ds(pl.multiple_of(g * LANES, LANES), LANES)
        cself[0:1, lanes] = self_overlap(confp, lanes, atoms)
        return carry

    selves = own_rows // LANES
    lax.fori_loop(0, selves, self_step, 0)

    z_rest = pl.ds(0, nz - 1)
    l_rest = pl.ds(0, nl - 1)
    d_rest = pl.ds(0, dev - 1)

    lib_copy.wait()
    blocks = own_rows // LANES
    turns = [n * blocks // nz for n in range(nz + 1)]

    def turn(n):
        for b in range(turns[n], turns[n + 1]):
            at = slice(b * LANES, (b + 1) * LANES)
            turned[:, at] = jnp.transpose(lib[at, :])

    turn(0)
    take(atoms_in.at[0, 0, z_rest], recv_a)
    for e in range(nl - 1, 0, -1):
        atoms_to(l, q, flip(l, e), send_b, recv_b).start()
    atoms_to(l, sib, l, send_e, recv_e).start()
    for d in range(1, nz):
        stage1(d).wait_recv()
        for e in range(nl - 1, 0, -1):
            stage2(d, e).start()
        to_sib(from_z(d), l, 0 if d < nz // 2 else 1).start()
        turn(d)

    take(codes_in.at[d_rest], recv_c)
    parts = [None] * groups
    for s in range(dev):
        g = cap * s // LANES
        for k in range(2):
            if g + k < groups:
                row = codes_in[s, k]
                parts[g + k] = row if parts[g + k] is None else parts[g + k] + row
    none = jnp.zeros((1, LANES), I32)
    pcode = jnp.concatenate([none if p is None else p for p in parts], axis=1)
    valid = pcode > 0
    pcode = jnp.maximum(pcode - 1, 0)
    pslot = fdiv(pcode, local_q)
    source = fdiv(iota((1, pairs), 1), cap)
    which = pcode - pslot * local_q
    pquery = source * local_q + which
    src_q, src_l = source // nl, source % nl
    held = ((src_l * CORES + src_q % CORES) * nz + src_q // CORES) * local_q + which
    onehot[...] = jnp.where(iota((own_rows, pairs), 0) == pslot, 1.0, 0.0).astype(BF16)
    qonehot[...] = jnp.where(iota((dev * local_q, pairs), 0) == held, 1.0, 0.0).astype(BF16)

    take(atoms_in.at[l_rest, 0], recv_b)
    for e in range(nl - 1, 0, -1):
        atoms_to(flip(l, e), sib, l, send_e, recv_e).start()

    self_hi, self_lo = split2(cself[...])
    pad = jnp.zeros((14, own_rows), BF16)
    found = nn(jnp.concatenate([conf[...].astype(BF16), self_hi, self_lo, pad], axis=0), onehot[...])
    comps = prepare(*(found[i * atoms : (i + 1) * atoms] for i in range(4)))
    for i in range(4):
        pairs_c[i * atoms : (i + 1) * atoms] = comps[i]
    pairs_c[4 * atoms : 4 * atoms + 1] = found[4 * atoms : 4 * atoms + 1] + found[4 * atoms + 1 : 4 * atoms + 2]

    take(atoms_in.at[:, 0], recv_e)
    raw = atoms_in[...].reshape(dev, 2 * local_q, LANES).astype(F32)
    q_top = jnp.transpose(raw[:, :local_q].reshape(dev * local_q, LANES))
    q_low = jnp.transpose(raw[:, local_q:].reshape(dev * local_q, LANES))
    found = nn(jnp.concatenate([q_top, q_low], axis=0).astype(BF16), qonehot[...])
    comps = prepare(
        found[:atoms], found[atoms:half], found[LANES : LANES + atoms], found[LANES + atoms : LANES + half]
    )
    for i in range(4):
        pairs_q[i * atoms : (i + 1) * atoms] = comps[i]
    own = LANES + half
    pairs_q[4 * atoms : 4 * atoms + 1] = found[own : own + 1] + found[own + 1 : own + 2]
    inverse = raw[:, local_q:, half + 2 : half + 3] + raw[:, local_q:, half + 3 : half + 4]
    inverse = 1.0 / (inverse + raw[:, local_q:, half + 4 : half + 5] + EPSILON)
    for s in range(dev):
        there = (s % nl * CORES + s // nl % CORES) * nz + s // nl // CORES
        inv_ref[s * local_q : (s + 1) * local_q, :] = inverse[there]

    def onward(late, n):
        d = 1 + lax.div(n, nl - 1)
        e = nl - 1 - lax.rem(n, nl - 1)
        stage2(d, e).wait_recv()
        to_sib(from_z(d), flip(l, e), late).start()

    def cross_step(late, first, last, start, each, g, carry):
        for k in range(each):
            n = first + (g - start) * each + k
            if (last - first) % each:
                pl.when(n < last)(functools.partial(onward, late, n))
            else:
                onward(late, n)
        lanes = pl.ds(pl.multiple_of(g * LANES, LANES), LANES)
        cross = cross_overlap(pairs_q, pairs_c, lanes, atoms)
        selves = pairs_q[4 * atoms : 4 * atoms + 1, lanes] + pairs_c[4 * atoms : 4 * atoms + 1, lanes]
        shape_s[0:1, lanes] = cross / (selves - cross)
        return carry

    def cross_groups(late, first, last, start, stop):
        each = (last - first + stop - start - 1) // (stop - start)
        stop_at = stop if each == 0 else start + (last - first + each - 1) // each
        step = functools.partial(cross_step, late, first, last, start, each)
        lax.fori_loop(start, stop_at, step, 0)
        if stop_at < stop:
            lax.fori_loop(stop_at, stop, functools.partial(cross_step, late, last, last, start, 0), 0)

    rows = nq * block
    chunk = min(rows, 256)

    n_near, n_far = (nz // 2 - 1) * (nl - 1), (nz - 1) * (nl - 1)
    cuts = (groups // 3, 2 * groups // 3)
    cross_groups(0, 0, n_near, 0, cuts[0])
    cross_groups(1, n_near, n_far, cuts[0], cuts[1])

    part_prints = gath.at[:, pl.ds(0, nz * block // 2), :]

    cross_groups(1, n_far, n_far, cuts[1], groups)

    take(part_prints, sib_recv.at[0])
    take(part_prints, sib_recv.at[1])
    for r in range(0, rows, chunk):
        at = slice(r, r + chunk)
        scores = None
        for k in range(nl):
            prod = nn(gath[k, at, :], turned[k * cols : (k + 1) * cols, :])
            scores = prod if scores is None else scores + prod
        tv_ref[at, :] = (scores * inv_ref[at, :]).astype(BF16)

    tv_copy = pltpu.make_async_copy(tv_ref, tv_hbm, loc_sem.at[7])
    tv_copy.start()
    for g in range(groups):
        first = LANES * g // cap * local_q // 16 * 16
        last = min((LANES * g + LANES - 1) // cap * local_q // 16 * 16 + 16, rows)
        lanes = slice(g * LANES, (g + 1) * LANES)
        chosen = nn(tv_ref[first:last, :], onehot[:, lanes])
        mine = iota((last - first, LANES), 0) + first == pquery[:, lanes]
        prior = jnp.sum(jnp.where(mine, chosen, 0.0), axis=0, keepdims=True)
        score[g] = jnp.where(valid[:, lanes], shape_s[:, lanes] + prior, 0.0)
    score[groups] = jnp.zeros((1, LANES), F32)

    for tq, tl in peers:
        at = lax.div(cap * (tq * nl + tl), LANES)
        remote(score.at[pl.ds(at, 2)], ret_in.at[me_o], send_d, recv_d, tq, tl).start()
    own_copy = pltpu.make_async_copy(score.at[pl.ds(lax.div(cap * me, LANES), 2)], ret_in.at[me_o], loc_sem.at[5])
    own_copy.start()

    take(gath.at[0, pl.ds(0, (nz - 1) * block), :], s1_send)
    take(gath.at[pl.ds(0, nl - 1), pl.ds(0, (nz - 1) * block), :], s2_send)
    take(gath.at[:, pl.ds(0, nz * block), :], sib_send)
    take(atoms_in.at[0, 0, z_rest], send_a)
    take(atoms_in.at[l_rest, 0], send_b)
    take(atoms_in.at[:, 0], send_e)
    take(codes_in.at[d_rest], send_c)
    tv_copy.wait()
    meta_copy.wait()
    own_copy.wait()
    take(ret_in.at[d_rest], recv_d)
    take(ret_in.at[d_rest], send_d)


def finish(tv_in, ret_in, meta, count, tv_out, out_ref, sem):
    copy = pltpu.make_async_copy(tv_in, tv_out, sem)
    copy.start()
    dev = ret_in.shape[0]
    local_q, listed = out_ref.shape
    cand_n = local_q * listed
    owns = iota((dev, cand_n), 0) == meta[0]
    rank_b = jnp.where(iota((2 * LANES, cand_n), 0) == meta[1], 1.0, 0.0).astype(BF16)
    came = jnp.concatenate([ret_in[:, k].reshape(dev, LANES) for k in range(2)], axis=1)
    hi_b, lo_b = split2(came)
    mine = nn(hi_b, rank_b) + nn(lo_b, rank_b)
    final = jnp.sum(jnp.where(owns, mine, 0.0), axis=0, keepdims=True)
    for i in range(local_q):
        line = final[:, i * listed : (i + 1) * listed]
        live = iota((1, listed), 1) < count[i]
        out_ref[i : i + 1, :] = jnp.where(live, line, 0.0)
    copy.wait()


def hand_over(tv, ret, meta, count, out_shape):
    vspec = pl.BlockSpec(memory_space=pltpu.VMEM)
    return pl.pallas_call(
        finish,
        out_shape=(jax.ShapeDtypeStruct(tv.shape, tv.dtype), jax.ShapeDtypeStruct(out_shape, F32)),
        in_specs=[vspec, vspec, vspec, pl.BlockSpec(memory_space=pltpu.SMEM)],
        out_specs=(pl.BlockSpec(memory_space=pl.ANY), vspec),
        scratch_shapes=[pltpu.SemaphoreType.DMA],
    )(tv, ret, meta, count)


def body(nq, nl, query_prints, library_prints, query_atoms, conformer_atoms, candidates, candidate_count, home_row):
    dev = nq * nl
    block, width = query_prints.shape
    own_rows = library_prints.shape[0]
    local_q, listed = candidates.shape
    atoms = query_atoms.shape[1] // 4
    cand_n = local_q * listed
    cap = 2 * ((cand_n + dev - 1) // dev) + 4
    pairs = (dev * cap + LANES - 1) // LANES * LANES
    id_bytes = ((home_row.shape[0] - 1).bit_length() + 7) // 8
    rows = nq * block
    nz = nq // CORES
    limit = 56 * 1024 * 1024
    vm = pltpu.VMEM
    dma = pltpu.SemaphoreType.DMA
    hspec = pl.BlockSpec(memory_space=pl.ANY)
    tv, ret, meta = pl.pallas_call(
        functools.partial(kernel, nq, nl, cap, id_bytes),
        out_shape=(
            jax.ShapeDtypeStruct((rows, own_rows), BF16),
            jax.ShapeDtypeStruct((dev, 2, 1, LANES), F32),
            jax.ShapeDtypeStruct((2, 1, cand_n), I32),
        ),
        in_specs=[pl.BlockSpec(memory_space=pltpu.HBM)] * 6,
        out_specs=(hspec, hspec, hspec),
        scratch_shapes=[
            vm((rows, own_rows), BF16),
            vm((block, width), BF16),
            vm((local_q, 4 * atoms), F32),
            vm((local_q, listed), I32),
            vm((home_row.shape[0] // LANES, LANES), I32),
            vm((own_rows, width), BF16),
            vm((width, own_rows), BF16),
            vm((4 * atoms, own_rows), F32),
            vm((nl, rows, width // nl), BF16),
            vm((2 * local_q, LANES), BF16),
            vm((nl, CORES, nz, 2 * local_q, LANES), BF16),
            vm((dev, 2, 1, LANES), I32),
            vm((dev, 2, 1, LANES), I32),
            vm((pairs // LANES + 1, 1, LANES), F32),
            vm((2, 1, cand_n), I32),
            vm((4 * atoms, own_rows), F32),
            vm((4 * atoms, LANES), F32),
            vm((4 * atoms + 8, pairs), F32),
            vm((4 * atoms + 8, pairs), F32),
            vm((rows, 1), F32),
            vm((own_rows, pairs), BF16),
            vm((rows, pairs), BF16),
            vm((1, own_rows), F32),
            vm((1, pairs), F32),
            dma((8,)),
            dma, dma((nz,)),
            dma, dma((2,)),
            dma, dma((nz, nl)),
            dma, dma, dma, dma, dma, dma, dma, dma, dma, dma,
            pltpu.SemaphoreType.REGULAR,
        ],
        compiler_params=pltpu.CompilerParams(
            collective_id=0, has_side_effects=True, vmem_limit_bytes=limit
        ),
    )(
        query_prints, library_prints, query_atoms, conformer_atoms.T, candidates,
        home_row.reshape(-1, LANES),
    )
    return hand_over(tv, ret, meta, candidate_count, (local_q, listed))


def solution(mesh):
    return jax.shard_map(
        functools.partial(body, mesh.shape["qry"], mesh.shape["lib"]),
        mesh=mesh,
        in_specs=(
            P("qry", None),
            P(("lib", "qry"), None),
            P(("qry", "lib"), None),
            P(("lib", "qry"), None),
            P(("qry", "lib"), None),
            P(("qry", "lib")),
            P(),
        ),
        out_specs=(P(None, ("lib", "qry")), P(("qry", "lib"), None)),
        check_vma=False,
    )
```

```python
import functools
import math

import jax
import jax.numpy as jnp
from jax import lax
from jax.experimental import pallas as pl
from jax.experimental.pallas import tpu as pltpu
from jax.sharding import PartitionSpec as P

SHARPNESS = 0.8
EPSILON = 1e-06
LANES = 128
CORES = 2
SCALE = SHARPNESS * math.log2(math.e)
ROOT = math.sqrt(2.0 * SCALE)

F32 = jnp.float32
BF16 = jnp.bfloat16
I32 = jnp.int32


def nt(a, b):
    return lax.dot_general(a, b, (((1,), (1,)), ((), ())), preferred_element_type=F32)


def nn(a, b):
    return lax.dot_general(a, b, (((1,), (0,)), ((), ())), preferred_element_type=F32)


def split2(x):
    hi = x.astype(BF16)
    return hi, (x - hi.astype(F32)).astype(BF16)


def iota(shape, dim):
    return lax.broadcasted_iota(I32, shape, dim)


def fdiv(x, by):
    return jnp.floor((x.astype(F32) + 0.5) * (1.0 / by)).astype(I32)


def prepare(x, y, z, w):
    norm = SCALE * (x * x + y * y + z * z)
    return x * ROOT, y * ROOT, z * ROOT, w * jnp.exp2(-norm)


def self_overlap(ref, lanes, atoms):
    blocks = atoms // 8
    comp = [[ref[pl.ds(c * atoms + 8 * i, 8), lanes] for i in range(blocks)] for c in range(4)]
    total = None
    diag = [None] * blocks
    off = [None] * blocks
    for a in range(atoms):
        xa, ya, za, wa = (ref[pl.ds(c * atoms + a, 1), lanes] for c in range(4))
        wa2 = wa + wa
        for i in range(a // 8, blocks):
            e = jnp.exp2(xa * comp[0][i] + ya * comp[1][i] + za * comp[2][i])
            if i == a // 8:
                diag[i] = wa * e if diag[i] is None else diag[i] + wa * e
            else:
                off[i] = wa2 * e if off[i] is None else off[i] + wa2 * e
    for i in range(blocks):
        part = diag[i] if off[i] is None else diag[i] + off[i]
        part = part * comp[3][i]
        total = part if total is None else total + part
    return jnp.sum(total, axis=0, keepdims=True)


def cross_overlap(qref, cref, lanes, atoms):
    comp = [cref[pl.ds(c * atoms, atoms), lanes] for c in range(4)]
    acc = None
    for a in range(atoms):
        xa, ya, za, wa = (qref[pl.ds(c * atoms + a, 1), lanes] for c in range(4))
        e = wa * jnp.exp2(xa * comp[0] + ya * comp[1] + za * comp[2])
        acc = e if acc is None else acc + e
    return jnp.sum(acc * comp[3], axis=0, keepdims=True)


def flip(x, bits):
    step, out = 1, x
    while step < 256:
        one = lax.rem(lax.div(x, step), 2)
        other = lax.rem(lax.div(bits, step), 2) if not isinstance(bits, int) else (bits // step) % 2
        out = out + other * (1 - 2 * one) * step
        step *= 2
        if isinstance(bits, int) and step > bits:
            break
    return out


def kernel(
    nq, nl, cap, id_bytes,
    qp_hbm, lib_hbm, qa_hbm, conf_hbm, cand_hbm, count_hbm, home_hbm,
    tv_hbm, ret_in, meta_hbm,
    tv_ref,
    qp_ref, qa_ref, cand_ref, count_ref, home_ref,
    lib, turned, conf, gath, pack, atoms_in, codes_out, codes_in, score, meta,
    confp, ownprep, pairs_c, pairs_q, inv_ref, onehot, qonehot, cself, shape_s,
    loc_sem, s1_send, s1_recv, sib_send, sib_recv, s2_send, s2_recv,
    send_a, recv_a, send_b, recv_b, send_c, recv_c, send_d, recv_d, send_e, recv_e, ready,
):
    q = lax.axis_index("qry")
    l = lax.axis_index("lib")
    dev = nq * nl
    me = q * nl + l
    me_o = l * nq + q
    nz = nq // CORES
    z, c = lax.div(q, CORES), lax.rem(q, CORES)
    sib = z * CORES + (1 - c)
    own_rows = lib.shape[0]
    block = qp_ref.shape[0]
    cols = gath.shape[2]
    local_q, listed = cand_ref.shape
    cand_n = local_q * listed
    atoms = qa_ref.shape[1] // 4
    half = 2 * atoms
    pairs = onehot.shape[1]
    groups = pairs // LANES

    spread = [(d, e) for d in range(nq) for e in range(nl) if d or e]
    spread.sort(key=lambda o: -(o[0] // CORES + bin(o[1]).count("1")))
    near = [(q, flip(l, e)) for e in range(nl - 1, 0, -1)] + [(flip(q, d), l) for d in range(nq - 1, 0, -1)]
    peers = [(flip(q, d) if d else q, flip(l, e) if e else l) for d, e in spread]

    def take(ref, sem):
        pltpu.make_async_copy(ref, ref, sem).wait()

    def remote(src, dst, ssem, rsem, dq, dl):
        return pltpu.make_async_remote_copy(
            src_ref=src, dst_ref=dst, send_sem=ssem, recv_sem=rsem,
            device_id={"qry": dq, "lib": dl}, device_id_type=pl.DeviceIdType.MESH,
        )

    barrier = pltpu.get_barrier_semaphore()
    loads = [
        pltpu.make_async_copy(src, dst, loc_sem.at[2 + n])
        for n, (src, dst) in enumerate(
            ((qa_hbm, qa_ref), (cand_hbm, cand_ref), (home_hbm, home_ref), (qp_hbm, qp_ref), (count_hbm, count_ref))
        )
    ]
    for load in loads:
        load.start()
    lib_copy = pltpu.make_async_copy(lib_hbm, lib, loc_sem.at[0])
    conf_copy = pltpu.make_async_copy(conf_hbm, conf, loc_sem.at[1])
    conf_copy.start()
    lib_copy.start()

    for tq, tl in near:
        pl.semaphore_signal(
            barrier, inc=1, device_id={"qry": tq, "lib": tl}, device_id_type=pl.DeviceIdType.MESH
        )

    loads[3].wait()
    loads[0].wait()

    qa = qa_ref[...]
    zero = jnp.zeros((local_q, LANES - half), F32)
    top = jnp.concatenate([qa[:, :half], zero], axis=1)
    low = jnp.concatenate([qa[:, half:], zero], axis=1)
    fill = jnp.zeros((LANES - local_q, LANES), F32)
    top_t = jnp.transpose(jnp.concatenate([top, fill], axis=0))
    low_t = jnp.transpose(jnp.concatenate([low, fill], axis=0))
    comps = prepare(top_t[:atoms], top_t[atoms:half], low_t[:atoms], low_t[atoms:half])
    for i in range(4):
        ownprep[i * atoms : (i + 1) * atoms] = comps[i]
    own_self = self_overlap(ownprep, pl.ds(0, LANES), atoms)
    lane_at = iota((local_q, LANES), 1)
    own_col = jnp.sum(
        jnp.where(lane_at == iota((local_q, LANES), 0), own_self, 0.0), axis=1, keepdims=True
    )
    own_hi = own_col.astype(BF16).astype(F32)
    prints = qp_ref[...].astype(F32)
    squares = jnp.sum(prints * prints, axis=1, keepdims=True)
    norm = jnp.zeros((local_q, 1), F32)
    for k in range(nl):
        norm = norm + jnp.where(l == k, squares[k * local_q : (k + 1) * local_q], 0.0)
    norm_hi = norm.astype(BF16).astype(F32)
    norm_mid = (norm - norm_hi).astype(BF16).astype(F32)
    extra = (own_hi, own_col - own_hi, norm_hi, norm_mid, norm - norm_hi - norm_mid)
    for k, column in enumerate(extra):
        low = jnp.where(lane_at == half + k, column, low)
    pack[...] = jnp.concatenate([top, low], axis=0).astype(BF16)

    pl.semaphore_wait(barrier, nq + nl - 2)
    for e in range(nl - 1, 0, -1):
        pl.semaphore_signal(
            ready, inc=1, device_id={"qry": q, "lib": flip(l, e)}, device_id_type=pl.DeviceIdType.MESH
        )

    def piece(bq, k):
        return gath.at[k, pl.ds(pl.multiple_of(bq * block, block), block), :]

    def from_z(d):
        return flip(z, d) * CORES + c

    def stage1(d):
        return remote(
            qp_ref.at[:, pl.ds(pl.multiple_of(l * cols, cols), cols)], piece(q, l),
            s1_send, s1_recv.at[d], from_z(d), l,
        )

    def stage2(d, e):
        there = piece(from_z(d), l)
        return remote(there, there, s2_send, s2_recv.at[d, e], q, flip(l, e))

    def to_sib(bq, k, late):
        there = piece(bq, k)
        return remote(there, there, sib_send, sib_recv.at[late], sib, l)

    def atoms_to(k, dq, dl, ssem, rsem):
        there = atoms_in.at[k, c]
        return remote(there, there, ssem, rsem, dq, dl)

    for d in range(nz - 1, 0, -1):
        remote(pack, atoms_in.at[l, c, z], send_a, recv_a, from_z(d), l).start()
    for d in range(1, nz):
        stage1(d).start()
    for k in range(nl):
        gath[k, pl.ds(pl.multiple_of(q * block, block), block), :] = qp_ref[:, k * cols : (k + 1) * cols]
    atoms_in[l, c, z] = pack[...]

    for load in loads[1:3] + loads[4:]:
        load.wait()

    ids = jnp.concatenate([cand_ref[pl.ds(i, 1), :] for i in range(local_q)], axis=1)
    table = home_ref[...]
    trows = table.shape[0]
    pieces = [
        jnp.transpose(((table >> (8 * k)) & 255).astype(F32)).astype(BF16) for k in range(id_bytes)
    ]
    row_hot = jnp.where(iota((trows, cand_n), 0) == (ids >> 7), 1.0, 0.0).astype(BF16)
    lane_hot = iota((LANES, cand_n), 0) == (ids & 127)
    stored = jnp.zeros((1, cand_n), I32)
    for k in range(id_bytes):
        found = nn(pieces[k], row_hot)
        byte = jnp.sum(jnp.where(lane_hot, found, 0.0), axis=0, keepdims=True)
        stored = stored + (byte.astype(I32) << (8 * k))
    owner = fdiv(stored, own_rows)
    slot = stored - owner * own_rows

    owns = iota((dev, cand_n), 0) == owner
    owns_b = jnp.where(owns, 1.0, 0.0).astype(BF16)
    tri = jnp.where(iota((cand_n, cand_n), 0) < iota((cand_n, cand_n), 1), 1.0, 0.0).astype(BF16)
    before = nn(owns_b, tri)
    rank = jnp.sum(jnp.where(owns, before, 0.0), axis=0, keepdims=True).astype(I32)
    my_off = lax.rem(cap * me, LANES)
    live = jnp.concatenate(
        [jnp.where(iota((1, listed), 1) < count_ref[i], 1, 0) for i in range(local_q)], axis=1
    )
    meta[0] = jnp.where(live > 0, owner, -1)
    meta[1] = rank + my_off
    meta_copy = pltpu.make_async_copy(meta, meta_hbm, loc_sem.at[8])
    meta_copy.start()
    rank_b = jnp.where(iota((2 * LANES, cand_n), 0) == rank + my_off, 1.0, 0.0).astype(BF16)
    code = slot * local_q + fdiv(iota((1, cand_n), 1), listed) + 1
    lo = (code & 127).astype(F32)
    hi = (code >> 7).astype(F32)
    left = jnp.concatenate([jnp.where(owns, lo, 0.0), jnp.where(owns, hi, 0.0)], axis=0).astype(BF16)
    sums = nt(left, rank_b).astype(I32)
    codes = sums[:dev] + (sums[dev:] << 7)
    for o in range(dev):
        for k in range(2):
            codes_out[o, k] = codes[o : o + 1, k * LANES : (k + 1) * LANES]

    pl.semaphore_wait(ready, nl - 1)
    for tq, tl in peers:
        remote(codes_out.at[tl * nq + tq], codes_in.at[me], send_c, recv_c, tq, tl).start()
    for k in range(nl):
        to_sib(q, k, 0).start()
    codes_in[me] = codes_out[me_o]

    conf_copy.wait()
    comps = prepare(*(conf[i * atoms : (i + 1) * atoms] for i in range(4)))
    for i in range(4):
        confp[i * atoms : (i + 1) * atoms] = comps[i]

    def self_step(g, carry):
        lanes = pl.ds(pl.multiple_of(g * LANES, LANES), LANES)
        cself[0:1, lanes] = self_overlap(confp, lanes, atoms)
        return carry

    selves = own_rows // LANES
    lax.fori_loop(0, selves, self_step, 0)

    z_rest = pl.ds(0, nz - 1)
    l_rest = pl.ds(0, nl - 1)
    d_rest = pl.ds(0, dev - 1)

    lib_copy.wait()
    blocks = own_rows // LANES
    turns = [n * blocks // nz for n in range(nz + 1)]

    def turn(n):
        for b in range(turns[n], turns[n + 1]):
            at = slice(b * LANES, (b + 1) * LANES)
            turned[:, at] = jnp.transpose(lib[at, :])

    turn(0)
    take(atoms_in.at[0, 0, z_rest], recv_a)
    for e in range(nl - 1, 0, -1):
        atoms_to(l, q, flip(l, e), send_b, recv_b).start()
    atoms_to(l, sib, l, send_e, recv_e).start()
    for d in range(1, nz):
        stage1(d).wait_recv()
        for e in range(nl - 1, 0, -1):
            stage2(d, e).start()
        to_sib(from_z(d), l, 0 if d < nz // 2 else 1).start()
        turn(d)

    take(codes_in.at[d_rest], recv_c)
    parts = [None] * groups
    for s in range(dev):
        g = cap * s // LANES
        for k in range(2):
            if g + k < groups:
                row = codes_in[s, k]
                parts[g + k] = row if parts[g + k] is None else parts[g + k] + row
    none = jnp.zeros((1, LANES), I32)
    pcode = jnp.concatenate([none if p is None else p for p in parts], axis=1)
    valid = pcode > 0
    pcode = jnp.maximum(pcode - 1, 0)
    pslot = fdiv(pcode, local_q)
    source = fdiv(iota((1, pairs), 1), cap)
    which = pcode - pslot * local_q
    pquery = source * local_q + which
    src_q, src_l = source // nl, source % nl
    held = ((src_l * CORES + src_q % CORES) * nz + src_q // CORES) * local_q + which
    onehot[...] = jnp.where(iota((own_rows, pairs), 0) == pslot, 1.0, 0.0).astype(BF16)
    qonehot[...] = jnp.where(iota((dev * local_q, pairs), 0) == held, 1.0, 0.0).astype(BF16)

    take(atoms_in.at[l_rest, 0], recv_b)
    for e in range(nl - 1, 0, -1):
        atoms_to(flip(l, e), sib, l, send_e, recv_e).start()

    self_hi, self_lo = split2(cself[...])
    pad = jnp.zeros((14, own_rows), BF16)
    found = nn(jnp.concatenate([conf[...].astype(BF16), self_hi, self_lo, pad], axis=0), onehot[...])
    comps = prepare(*(found[i * atoms : (i + 1) * atoms] for i in range(4)))
    for i in range(4):
        pairs_c[i * atoms : (i + 1) * atoms] = comps[i]
    pairs_c[4 * atoms : 4 * atoms + 1] = found[4 * atoms : 4 * atoms + 1] + found[4 * atoms + 1 : 4 * atoms + 2]

    take(atoms_in.at[:, 0], recv_e)
    raw = atoms_in[...].reshape(dev, 2 * local_q, LANES).astype(F32)
    q_top = jnp.transpose(raw[:, :local_q].reshape(dev * local_q, LANES))
    q_low = jnp.transpose(raw[:, local_q:].reshape(dev * local_q, LANES))
    found = nn(jnp.concatenate([q_top, q_low], axis=0).astype(BF16), qonehot[...])
    comps = prepare(
        found[:atoms], found[atoms:half], found[LANES : LANES + atoms], found[LANES + atoms : LANES + half]
    )
    for i in range(4):
        pairs_q[i * atoms : (i + 1) * atoms] = comps[i]
    own = LANES + half
    pairs_q[4 * atoms : 4 * atoms + 1] = found[own : own + 1] + found[own + 1 : own + 2]
    inverse = raw[:, local_q:, half + 2 : half + 3] + raw[:, local_q:, half + 3 : half + 4]
    inverse = 1.0 / (inverse + raw[:, local_q:, half + 4 : half + 5] + EPSILON)
    for s in range(dev):
        there = (s % nl * CORES + s // nl % CORES) * nz + s // nl // CORES
        inv_ref[s * local_q : (s + 1) * local_q, :] = inverse[there]

    def onward(late, n):
        d = 1 + lax.div(n, nl - 1)
        e = nl - 1 - lax.rem(n, nl - 1)
        stage2(d, e).wait_recv()
        to_sib(from_z(d), flip(l, e), late).start()

    def cross_step(late, first, last, start, each, g, carry):
        for k in range(each):
            n = first + (g - start) * each + k
            if (last - first) % each:
                pl.when(n < last)(functools.partial(onward, late, n))
            else:
                onward(late, n)
        lanes = pl.ds(pl.multiple_of(g * LANES, LANES), LANES)
        cross = cross_overlap(pairs_q, pairs_c, lanes, atoms)
        selves = pairs_q[4 * atoms : 4 * atoms + 1, lanes] + pairs_c[4 * atoms : 4 * atoms + 1, lanes]
        shape_s[0:1, lanes] = cross / (selves - cross)
        return carry

    def cross_groups(late, first, last, start, stop):
        each = (last - first + stop - start - 1) // (stop - start)
        stop_at = stop if each == 0 else start + (last - first + each - 1) // each
        step = functools.partial(cross_step, late, first, last, start, each)
        lax.fori_loop(start, stop_at, step, 0)
        if stop_at < stop:
            lax.fori_loop(stop_at, stop, functools.partial(cross_step, late, last, last, start, 0), 0)

    rows = nq * block
    chunk = min(rows, 256)

    n_near, n_far = (nz // 2 - 1) * (nl - 1), (nz - 1) * (nl - 1)
    cuts = (groups // 3, 2 * groups // 3)
    cross_groups(0, 0, n_near, 0, cuts[0])
    cross_groups(1, n_near, n_far, cuts[0], cuts[1])

    part_prints = gath.at[:, pl.ds(0, nz * block // 2), :]

    cross_groups(1, n_far, n_far, cuts[1], groups)

    take(part_prints, sib_recv.at[0])
    take(part_prints, sib_recv.at[1])
    for r in range(0, rows, chunk):
        at = slice(r, r + chunk)
        part = jnp.concatenate([gath[k, at, :] for k in range(nl)], axis=1)
        for n in range(0, own_rows, 2 * LANES):
            wide = slice(n, n + 2 * LANES)
            tv_ref[at, wide] = (nn(part, turned[:, wide]) * inv_ref[at, :]).astype(BF16)

    tv_copy = pltpu.make_async_copy(tv_ref, tv_hbm, loc_sem.at[7])
    tv_copy.start()
    for g in range(groups):
        first = LANES * g // cap * local_q // 16 * 16
        last = min((LANES * g + LANES - 1) // cap * local_q // 16 * 16 + 16, rows)
        lanes = slice(g * LANES, (g + 1) * LANES)
        chosen = nn(tv_ref[first:last, :], onehot[:, lanes])
        mine = iota((last - first, LANES), 0) + first == pquery[:, lanes]
        prior = jnp.sum(jnp.where(mine, chosen, 0.0), axis=0, keepdims=True)
        score[g] = jnp.where(valid[:, lanes], shape_s[:, lanes] + prior, 0.0)
    score[groups] = jnp.zeros((1, LANES), F32)

    for tq, tl in peers:
        at = lax.div(cap * (tq * nl + tl), LANES)
        remote(score.at[pl.ds(at, 2)], ret_in.at[me_o], send_d, recv_d, tq, tl).start()
    own_copy = pltpu.make_async_copy(score.at[pl.ds(lax.div(cap * me, LANES), 2)], ret_in.at[me_o], loc_sem.at[1])
    own_copy.start()

    take(gath.at[0, pl.ds(0, (nz - 1) * block), :], s1_send)
    take(gath.at[pl.ds(0, nl - 1), pl.ds(0, (nz - 1) * block), :], s2_send)
    take(gath.at[:, pl.ds(0, nz * block), :], sib_send)
    take(atoms_in.at[0, 0, z_rest], send_a)
    take(atoms_in.at[l_rest, 0], send_b)
    take(atoms_in.at[:, 0], send_e)
    take(codes_in.at[d_rest], send_c)
    tv_copy.wait()
    meta_copy.wait()
    own_copy.wait()
    take(ret_in.at[d_rest], recv_d)
    take(ret_in.at[d_rest], send_d)


def finish(tv_in, ret_in, meta, tv_out, out_hbm, out_ref, sems):
    copy = pltpu.make_async_copy(tv_in, tv_out, sems.at[0])
    copy.start()
    dev = ret_in.shape[0]
    local_q, listed = out_ref.shape
    cand_n = local_q * listed
    owns = iota((dev, cand_n), 0) == meta[0]
    rank_b = jnp.where(iota((2 * LANES, cand_n), 0) == meta[1], 1.0, 0.0).astype(BF16)
    came = jnp.concatenate([ret_in[:, k].reshape(dev, LANES) for k in range(2)], axis=1)
    hi_b, lo_b = split2(came)
    mine = nn(jnp.concatenate([hi_b, lo_b], axis=0), rank_b)
    final = jnp.sum(jnp.where(owns, mine[:dev] + mine[dev:], 0.0), axis=0, keepdims=True)
    for i in range(local_q):
        out_ref[i : i + 1, :] = final[:, i * listed : (i + 1) * listed]
    last = pltpu.make_async_copy(out_ref, out_hbm, sems.at[1])
    last.start()
    last.wait()
    copy.wait()


def hand_over(tv, ret, meta, out_shape):
    vspec = pl.BlockSpec(memory_space=pltpu.VMEM)
    return pl.pallas_call(
        finish,
        out_shape=(jax.ShapeDtypeStruct(tv.shape, tv.dtype), jax.ShapeDtypeStruct(out_shape, F32)),
        in_specs=[vspec] * 3,
        out_specs=(pl.BlockSpec(memory_space=pl.ANY), pl.BlockSpec(memory_space=pl.ANY)),
        scratch_shapes=[pltpu.VMEM(out_shape, F32), pltpu.SemaphoreType.DMA((2,))],
    )(tv, ret, meta)


def body(nq, nl, query_prints, library_prints, query_atoms, conformer_atoms, candidates, candidate_count, home_row):
    dev = nq * nl
    block, width = query_prints.shape
    own_rows = library_prints.shape[0]
    local_q, listed = candidates.shape
    atoms = query_atoms.shape[1] // 4
    cand_n = local_q * listed
    cap = 2 * ((cand_n + dev - 1) // dev) + 4
    pairs = (dev * cap + LANES - 1) // LANES * LANES
    id_bytes = ((home_row.shape[0] - 1).bit_length() + 7) // 8
    rows = nq * block
    nz = nq // CORES
    limit = 56 * 1024 * 1024
    vm = pltpu.VMEM
    dma = pltpu.SemaphoreType.DMA
    hspec = pl.BlockSpec(memory_space=pl.ANY)
    tv, ret, meta = pl.pallas_call(
        functools.partial(kernel, nq, nl, cap, id_bytes),
        out_shape=(
            jax.ShapeDtypeStruct((rows, own_rows), BF16),
            jax.ShapeDtypeStruct((dev, 2, 1, LANES), F32),
            jax.ShapeDtypeStruct((2, 1, cand_n), I32),
        ),
        in_specs=[pl.BlockSpec(memory_space=pltpu.HBM)] * 7,
        out_specs=(hspec, hspec, hspec),
        scratch_shapes=[
            vm((rows, own_rows), BF16),
            vm((block, width), BF16),
            vm((local_q, 4 * atoms), F32),
            vm((local_q, listed), I32),
            pltpu.SMEM((local_q,), I32),
            vm((home_row.shape[0] // LANES, LANES), I32),
            vm((own_rows, width), BF16),
            vm((width, own_rows), BF16),
            vm((4 * atoms, own_rows), F32),
            vm((nl, rows, width // nl), BF16),
            vm((2 * local_q, LANES), BF16),
            vm((nl, CORES, nz, 2 * local_q, LANES), BF16),
            vm((dev, 2, 1, LANES), I32),
            vm((dev, 2, 1, LANES), I32),
            vm((pairs // LANES + 1, 1, LANES), F32),
            vm((2, 1, cand_n), I32),
            vm((4 * atoms, own_rows), F32),
            vm((4 * atoms, LANES), F32),
            vm((4 * atoms + 8, pairs), F32),
            vm((4 * atoms + 8, pairs), F32),
            vm((rows, 1), F32),
            vm((own_rows, pairs), BF16),
            vm((rows, pairs), BF16),
            vm((1, own_rows), F32),
            vm((1, pairs), F32),
            dma((9,)),
            dma, dma((nz,)),
            dma, dma((2,)),
            dma, dma((nz, nl)),
            dma, dma, dma, dma, dma, dma, dma, dma, dma, dma,
            pltpu.SemaphoreType.REGULAR,
        ],
        compiler_params=pltpu.CompilerParams(
            collective_id=0, has_side_effects=True, vmem_limit_bytes=limit
        ),
    )(
        query_prints, library_prints, query_atoms, conformer_atoms.T, candidates, candidate_count,
        home_row.reshape(-1, LANES),
    )
    return hand_over(tv, ret, meta, (local_q, listed))


def solution(mesh):
    return jax.shard_map(
        functools.partial(body, mesh.shape["qry"], mesh.shape["lib"]),
        mesh=mesh,
        in_specs=(
            P("qry", None),
            P(("lib", "qry"), None),
            P(("qry", "lib"), None),
            P(("lib", "qry"), None),
            P(("qry", "lib"), None),
            P(("qry", "lib")),
            P(),
        ),
        out_specs=(P(None, ("lib", "qry")), P(("qry", "lib"), None)),
        check_vma=False,
    )
```
